256 devices in a mesh: group: 8 (over y, core), member: 32 (over x, z).
Axes of the slice: x: 4, y: 4, z: 8, core: 2. Of those that a mesh axis runs over, the one named last changes fastest.
Arguments:
- histories: bfloat16 [131072, 1024], P(('group', 'member')), may hold values from -24 to 24
- lengths: int32 [512], P(('group', 'member')), may hold values from 0 to 384, as said below
- cotangent: bfloat16 [131072, 512], P(('group', 'member')), may hold values from -6 to 6
- w_in: bfloat16 [1024, 2048], replicated, may hold values from -0.1875 to 0.1875
Outputs:
- grad_histories: bfloat16 [131072, 1024], P(('group', 'member'))
- grad_w_in: float32 [1024, 2048], P('member')
The draws below stay inside these ranges and needn't reach their ends.
Inputs may be any that keep to these rules, and one draw needn't show every extreme that they name: `lengths`: with each history rounded up to whole blocks of 128 rows, a device's 2 histories take at most 4 blocks; in every group some device takes all 4.
All inputs are finite; a program needn't handle non-finite values.
Results may differ from the reference program's by a relative error of at most 0.0071.
Values may be sent and summed in bfloat16 or wider, within the bound.
No kernel may reach another device: no remote copies, remote signals or barrier semaphores. Data moves between devices by JAX's collectives and lax.ppermute only.
A program may use at most 128 MiB of HBM per device.

```python
import jax
import jax.numpy as jnp
from jax import lax

D = 1024
HEADS = 4
BLOCK = 128
NB = 4
SEQ_DEV = 2
HD = 512
ROWS = 131072
N_MEMBER = 32
DEVICES = 256


def draw_lengths(key, part):
    key = jax.random.fold_in(key, 7)
    keys = jax.random.split(key, 5)
    groups = DEVICES // N_MEMBER
    first = 1 + (jax.random.randint(keys[0], (DEVICES,), 0, 4) == 0).astype(jnp.int32)
    second = jax.random.randint(keys[1], (DEVICES,), 0, 2)
    chosen = jax.random.randint(keys[2], (groups,), 0, N_MEMBER)
    member_index = jnp.arange(DEVICES, dtype=jnp.int32) % N_MEMBER
    full = member_index == jnp.repeat(chosen, N_MEMBER)
    first = jnp.where(full, NB - 1, first)
    second = jnp.where(full, 1, second)
    tail_one = jax.random.randint(keys[3], (DEVICES,), 1, BLOCK + 1)
    tail_two = jax.random.randint(keys[4], (DEVICES,), 1, BLOCK + 1)
    tail_one = jnp.where(full, BLOCK, tail_one)
    len_one = (first - 1) * BLOCK + tail_one
    len_two = jnp.where(second > 0, (second - 1) * BLOCK + tail_two, 0)
    return jnp.stack([len_one, len_two], axis=1).reshape(-1).astype(jnp.int32)


def with_spikes(result, rng, source, target, blocks, factor):
    owner, partner = [(jnp.arange(result.shape[dim]) // (result.shape[dim] // blocks)).reshape([-1 if axis == dim else 1 for axis in range(result.ndim)]) for dim in (source, target)]
    chosen = jax.random.permutation(rng, blocks)[partner]
    strong = (owner == chosen) | (owner == (partner + blocks // 2) % blocks)
    return jnp.where(strong, factor * result, result)


def level_of(own_key, dims, cuts, low, largest):
    loudness, own = 1.0, jax.random.fold_in(own_key, 6)
    for dim, blocks in cuts:
        draws = jnp.exp(jax.random.uniform(jax.random.fold_in(own, dim), (blocks,), jnp.float32, low / len(cuts), largest / len(cuts)))
        loudness = loudness * jnp.repeat(draws, dims[dim] // blocks).reshape([-1 if axis == dim else 1 for axis in range(len(dims))])
    return loudness


def normal_values(key, extent, scale, most, shards=(), kind=jnp.bfloat16):
    gain = level_of(key, extent, shards, -0.22, 0.18) if shards else 1.0
    result = jax.random.normal(key, extent, jnp.float32) * scale * gain
    return jnp.minimum(jnp.maximum(result, -most), most).astype(kind)


def noise_with(stream_key, extent, deviation, most, cuts, heavy, held_as=jnp.bfloat16):
    result = deviation * jax.random.normal(stream_key, extent, jnp.float32)
    if cuts:
        result = result * level_of(stream_key, extent, cuts, -0.22, 0.18)
    return jnp.clip(with_spikes(result, jax.random.fold_in(stream_key, 3), *heavy), -most, most).astype(held_as)


def setup_inputs(seed: int = 0) -> dict:
    seeds = jax.random.split(jax.random.key(seed), 5)
    histories = noise_with(seeds[0], (ROWS, D), 1.0, 24.0, ((0, 256),), (0, 1, 256, 6.0))
    lengths = draw_lengths(jax.random.fold_in(seeds[4], 71), 0)
    cotangent = normal_values(seeds[2], (ROWS, HD), 1.0, 6.0, ((0, 256),))
    w_in = normal_values(seeds[3], (D, 4 * HD), D ** -0.5, 0.1875)
    return {"histories": histories, "lengths": lengths, "cotangent": cotangent, "w_in": w_in}


def layout(lens, rows, block):
    blocks = (lens + block - 1) // block
    start = jnp.concatenate([jnp.zeros((1,), jnp.int32), (jnp.cumsum(blocks) * block)[:-1].astype(jnp.int32)])
    row_index = jnp.arange(rows, dtype=jnp.int32)
    offset = row_index[:, None] - start[None, :]
    inside = (offset >= 0) & (offset < lens[None, :])
    live = jnp.any(inside, axis=1)
    slots = jnp.arange(lens.shape[0], dtype=jnp.int32)
    history = lax.optimization_barrier(jnp.sum(jnp.where(inside, slots[None, :], 0), axis=1)).astype(jnp.int32)
    position = lax.optimization_barrier(jnp.sum(jnp.where(inside, offset, 0), axis=1)).astype(jnp.int32)
    count = lax.optimization_barrier(jnp.sum(jnp.where(inside, lens[None, :], 0), axis=1)).astype(jnp.int32)
    used = jnp.sum(blocks).astype(jnp.int32)
    return (history, position, live, count, used)

def attend(uvqk, history, position, live, count, heads):
    rows = uvqk.shape[0]
    width = uvqk.shape[1] // 4
    size = width // heads
    parts = uvqk.astype(jnp.float32)
    gate_u = parts[:, :width]
    values = parts[:, width:2 * width].reshape(rows, heads, size)
    queries = parts[:, 2 * width:3 * width].reshape(rows, heads, size)
    keys = parts[:, 3 * width:].reshape(rows, heads, size)
    scores = jnp.einsum('qhd,khd->hqk', queries, keys, precision=lax.Precision.HIGHEST) * size ** (-0.5)
    valid = (history[:, None] == history[None, :]) & (position[None, :] <= position[:, None])
    valid = valid & live[:, None] & live[None, :]
    inverse = 1.0 / jnp.maximum(count, 1).astype(jnp.float32)
    weights = jax.nn.silu(scores) * valid[None].astype(jnp.float32) * inverse[None, :, None]
    attended = jnp.einsum('hqk,khd->qhd', weights, values, precision=lax.Precision.HIGHEST).reshape(rows, width)
    centred = attended - lax.optimization_barrier(jnp.mean(attended, axis=1, keepdims=True))
    spread = lax.optimization_barrier(jnp.mean(centred * centred, axis=1, keepdims=True))
    return centred * lax.rsqrt(spread + 1e-05) * gate_u

def pull_back(uvqk, cotangent, history, position, live, count, heads):

    def local(table):
        return attend(table, history, position, live, count, heads)
    _, pull = jax.vjp(local, uvqk)
    upstream = cotangent.astype(jnp.float32) * live[:, None].astype(jnp.float32)
    return pull(upstream)[0]

def silu_slope(h):
    sig = jax.nn.sigmoid(h)
    return sig * (1.0 + h * (1.0 - sig))

def device_terms(x_rows, dy_rows, lens, w_in):
    history, position, live, count, used = layout(lens, x_rows.shape[0], BLOCK)
    h = jnp.dot(x_rows, w_in, preferred_element_type=jnp.float32)
    uvqk = jax.nn.silu(h).astype(jnp.bfloat16)
    grad_uvqk = pull_back(uvqk, dy_rows, history, position, live, count, HEADS)
    grad_h = (grad_uvqk.astype(jnp.float32) * silu_slope(h)).astype(jnp.bfloat16)
    grad_x = lax.dot_general(grad_h, w_in, (((1,), (1,)), ((), ())), preferred_element_type=jnp.float32).astype(jnp.bfloat16)
    grad_w = lax.dot_general(x_rows, grad_h, (((0,), (0,)), ((), ())), preferred_element_type=jnp.float32)
    return (grad_x, grad_w)

def reference(histories, lengths, cotangent, w_in):
    rows = BLOCK * NB
    xs = histories.reshape(DEVICES, rows, D)
    dys = cotangent.reshape(DEVICES, rows, HD)
    lens = lengths.reshape(DEVICES, SEQ_DEV)

    def step(total, item):
        grad_x, grad_w = device_terms(item[0], item[1], item[2], w_in)
        return (total + grad_w, grad_x)
    total, grads = lax.scan(step, jnp.zeros((D, 4 * HD), jnp.float32), (xs, dys, lens))
    return (grads.reshape(DEVICES * rows, D), total)
```

```python
import jax
import jax.numpy as jnp
from jax import lax
from jax.sharding import PartitionSpec as P
from jax.experimental import pallas as pl
from jax.experimental.pallas import tpu as pltpu

HEADS = 4
BLOCK = 128
NT = (((1,), (1,)), ((), ()))
TN = (((0,), (0,)), ((), ()))


def mm(a, b, dims=(((1,), (0,)), ((), ()))):
    return lax.dot_general(a, b, dims, preferred_element_type=jnp.float32)


def grads_kernel(core_ref, len_ref, x_ref, w_hbm, cot_ref, keep_ref, send_ref,
                 w_ref, slope_ref, act_ref, p_ref, s_ref, att_ref, da_ref, g_ref, sems):
    rows, width = cot_ref.shape
    nblocks = rows // BLOCK
    size = width // HEADS
    half = width // 2
    scale = size ** -0.5
    order = (2, 3, 1, 0)
    copies = {}
    for s in order:
        cols = pl.ds(s * width, width)
        copies[s] = pltpu.make_async_copy(w_hbm.at[:, cols], w_ref.at[:, cols], sems.at[s])
        copies[s].start()
    for s in order:
        copies[s].wait()
        for i in range(2):
            r = pl.ds(i * (rows // 2), rows // 2)
            cols = pl.ds(s * width, width)
            h = mm(x_ref[r, :], w_ref[:, cols])
            sig = 0.5 * jnp.tanh(0.5 * h) + 0.5
            act = h * sig
            act_ref[r, cols] = act.astype(jnp.bfloat16)
            slope_ref[r, cols] = sig + act * (1.0 - sig)

    def col(s, h):
        return pl.ds(s * width + h * size, size)

    core = core_ref[0]

    def put(s, h, r, grad):
        value = grad.astype(jnp.bfloat16).astype(jnp.float32) * slope_ref[r, col(s, h)]
        to = s * half + (h % (HEADS // 2)) * size
        g_ref[(h // (HEADS // 2)) ^ core, r, pl.ds(to, size)] = value.astype(jnp.bfloat16)

    l0 = len_ref[0]
    l1 = len_ref[1]
    start1 = ((l0 + (BLOCK - 1)) // BLOCK) * BLOCK
    for i in range(nblocks):
        first = max(0, i - 2)
        span = i + 1 - first
        r = pl.ds(i * BLOCK, BLOCK)
        keys = pl.ds(first * BLOCK, span * BLOCK)
        row = i * BLOCK + lax.broadcasted_iota(jnp.int32, (BLOCK, 1), 0)
        in0 = row < l0
        in1 = (row >= start1) & (row < start1 + l1)
        low = jnp.where(in1, start1, 0)
        high = jnp.where(in0 | in1, row, -1)
        count = jnp.where(in0, l0, jnp.where(in1, l1, 1))
        inv = 1.0 / count.astype(jnp.float32)
        live = in0 | in1
        c = first * BLOCK + lax.broadcasted_iota(jnp.int32, (BLOCK, span * BLOCK), 1)
        valid = (c >= low) & (c <= high)
        for h in range(HEADS):
            t = mm(act_ref[r, col(2, h)], act_ref[keys, col(3, h)], NT)
            sig = 0.5 * jnp.tanh(t * (0.5 * scale)) + 0.5
            p = t * scale * sig
            p_b = jnp.where(valid, p, 0.0).astype(jnp.bfloat16)
            p_ref[h, r, keys] = p_b
            s_ref[h, r, keys] = jnp.where(valid, sig + p * (1.0 - sig), 0.0)
            att_ref[r, pl.ds(h * size, size)] = mm(p_b, act_ref[keys, col(1, h)]) * inv
        att = att_ref[r, :]
        cen = att - jnp.mean(att, axis=1, keepdims=True)
        rstd = lax.rsqrt(jnp.mean(cen * cen, axis=1, keepdims=True) + 1e-05)
        z = cen * rstd
        up = jnp.where(live, cot_ref[r, :].astype(jnp.float32), 0.0)
        du = up * z
        dz = up * act_ref[r, pl.ds(0, width)].astype(jnp.float32)
        m1 = jnp.mean(dz, axis=1, keepdims=True)
        m2 = jnp.mean(dz * z, axis=1, keepdims=True)
        da = (dz - m1 - z * m2) * (rstd * inv)
        da_ref[r, :] = da.astype(jnp.bfloat16)
        for h in range(HEADS):
            put(0, h, r, du[:, h * size:(h + 1) * size])
        for h in range(HEADS):
            dp = mm(da_ref[r, pl.ds(h * size, size)], act_ref[keys, col(1, h)], NT)
            ds = (dp * s_ref[h, r, keys]).astype(jnp.bfloat16)
            s_ref[h, r, keys] = ds.astype(jnp.float32)
            put(2, h, r, mm(ds, act_ref[keys, col(3, h)]) * scale)
    for j in range(nblocks):
        last = min(nblocks, j + 3)
        r = pl.ds(j * BLOCK, BLOCK)
        qs = pl.ds(j * BLOCK, (last - j) * BLOCK)
        for h in range(HEADS):
            put(1, h, r, mm(p_ref[h, qs, r], da_ref[qs, pl.ds(h * size, size)], TN))
            ds = s_ref[h, qs, r].astype(jnp.bfloat16)
            put(3, h, r, mm(ds, act_ref[qs, col(2, h)], TN) * scale)
    keep_ref[...] = g_ref[0]
    send_ref[...] = g_ref[1]


def grads(core, lengths, x, w, cot):
    rows, d = x.shape
    width = cot.shape[1]
    wide = w.shape[1]
    vmem = pl.BlockSpec(memory_space=pltpu.VMEM)
    smem = pl.BlockSpec(memory_space=pltpu.SMEM)
    return pl.pallas_call(
        grads_kernel,
        out_shape=[jax.ShapeDtypeStruct((rows, wide // 2), jnp.bfloat16)] * 2,
        in_specs=[smem, smem, vmem, pl.BlockSpec(memory_space=pl.ANY), vmem],
        out_specs=[vmem, vmem],
        scratch_shapes=[
            pltpu.VMEM((d, wide), jnp.bfloat16),
            pltpu.VMEM((rows, wide), jnp.float32),
            pltpu.VMEM((rows, wide), jnp.bfloat16),
            pltpu.VMEM((HEADS, rows, rows), jnp.bfloat16),
            pltpu.VMEM((HEADS, rows, rows), jnp.float32),
            pltpu.VMEM((rows, width), jnp.float32),
            pltpu.VMEM((rows, width), jnp.bfloat16),
            pltpu.VMEM((2, rows, wide // 2), jnp.bfloat16),
            pltpu.SemaphoreType.DMA((4,)),
        ],
        compiler_params=pltpu.CompilerParams(vmem_limit_bytes=40 * 2**20),
        cost_estimate=pl.CostEstimate(flops=4 * 10**9, bytes_accessed=8 * 10**6, transcendentals=2 * 10**6),
        name="uvqk_grads",
    )(core, lengths, x, w, cot)


def transpose_kernel(x_ref, y_ref, xt_ref):
    rows, d = x_ref.shape
    for i, ref in enumerate((x_ref, y_ref)):
        for b in range(0, d, 256):
            for r in range(0, rows, 256):
                xt_ref[pl.ds(b, 256), pl.ds(i * rows + r, 256)] = ref[pl.ds(r, 256), pl.ds(b, 256)].T


def transposed(x, y):
    rows, d = x.shape
    vmem = pl.BlockSpec(memory_space=pltpu.VMEM)
    return pl.pallas_call(
        transpose_kernel,
        out_shape=jax.ShapeDtypeStruct((d, 2 * rows), jnp.bfloat16),
        in_specs=[vmem, vmem],
        out_specs=vmem,
        compiler_params=pltpu.CompilerParams(vmem_limit_bytes=16 * 2**20),
        cost_estimate=pl.CostEstimate(flops=0, bytes_accessed=4 * 2**20, transcendentals=0),
        name="transpose_rows",
    )(x, y)


def weights_kernel(where_ref, xt_ref, keep_ref, recv_ref, o0, o1, o2, o3):
    core, first, second = where_ref[0], where_ref[1], where_ref[2]
    rows = keep_ref.shape[0]
    for k, out in enumerate((o0, o1, o2, o3)):
        for l in range(4):
            a = lax.rem(first + k, 4)
            b = lax.rem(second + l, 4)
            rb = jnp.where(core == 0, a, b)
            cb = jnp.where(core == 0, b, a)
            rs = pl.ds(pl.multiple_of(rb * 256, 256), 256)
            cs = pl.ds(pl.multiple_of(cb * 256, 256), 256)
            total = mm(xt_ref[rs, pl.ds(0, rows)], keep_ref[:, cs])
            total += mm(xt_ref[rs, pl.ds(rows, rows)], recv_ref[:, cs])
            out[l] = total.astype(jnp.bfloat16)


def weights(where, xt, keep, recv):
    vmem = pl.BlockSpec(memory_space=pltpu.VMEM)
    smem = pl.BlockSpec(memory_space=pltpu.SMEM)
    return pl.pallas_call(
        weights_kernel,
        out_shape=[jax.ShapeDtypeStruct((4, 256, 256), jnp.bfloat16)] * 4,
        in_specs=[smem, vmem, vmem, vmem],
        out_specs=[vmem] * 4,
        compiler_params=pltpu.CompilerParams(vmem_limit_bytes=24 * 2**20),
        cost_estimate=pl.CostEstimate(flops=2 * 2**30, bytes_accessed=6 * 2**20, transcendentals=0),
        name="weight_grads",
    )(where, xt, keep, recv)


def rows_kernel(core_ref, keep_ref, send_ref, w_ref, out_ref):
    core = core_ref[0]
    rows = keep_ref.shape[0]
    for r in range(0, rows, 256):
        total = jnp.zeros((256, w_ref.shape[0]), jnp.float32)
        for i, ref in enumerate((keep_ref, send_ref)):
            for s in range(4):
                cols = pl.ds(pl.multiple_of(s * 512 + (core ^ i) * 256, 256), 256)
                total += mm(ref[pl.ds(r, 256), pl.ds(s * 256, 256)], w_ref[:, cols], NT)
        out_ref[pl.ds(r, 256), :] = total.astype(jnp.bfloat16)


def row_grads(core, keep, send, w):
    vmem = pl.BlockSpec(memory_space=pltpu.VMEM)
    smem = pl.BlockSpec(memory_space=pltpu.SMEM)
    return pl.pallas_call(
        rows_kernel,
        out_shape=jax.ShapeDtypeStruct((keep.shape[0], w.shape[0]), jnp.bfloat16),
        in_specs=[smem, vmem, vmem, vmem],
        out_specs=vmem,
        compiler_params=pltpu.CompilerParams(vmem_limit_bytes=24 * 2**20),
        cost_estimate=pl.CostEstimate(flops=2 * 2**30, bytes_accessed=7 * 2**20, transcendentals=0),
        name="row_grads",
    )(core, keep, send, w)


def place_kernel(where_ref, mine_ref, other_ref, out_ref):
    core, y = where_ref[0], where_ref[3]
    for i, ref in enumerate((mine_ref, other_ref)):
        for k in range(4):
            s = lax.rem(y + 4 - k, 4)
            cols = pl.ds(pl.multiple_of(s * 512 + (core ^ i) * 256, 256), 256)
            out_ref[:, cols] = ref[k]


def place(where, mine, other):
    vmem = pl.BlockSpec(memory_space=pltpu.VMEM)
    smem = pl.BlockSpec(memory_space=pltpu.SMEM)
    return pl.pallas_call(
        place_kernel,
        out_shape=jax.ShapeDtypeStruct((mine.shape[1], 2048), jnp.float32),
        in_specs=[smem, vmem, vmem],
        out_specs=vmem,
        name="place_columns",
    )(where, mine, other)


AXES = ("group", "member")
NY, NX, NZ = 4, 4, 8


def pairs(move):
    out = []
    for i in range(2 * NY * NX * NZ):
        g, m = divmod(i, NX * NZ)
        y, c = divmod(g, 2)
        x, z = divmod(m, NZ)
        y, c, x, z = move(y, c, x, z)
        out.append((i, ((y % NY) * 2 + c % 2) * NX * NZ + (x % NX) * NZ + z % NZ))
    return out


def permute(value, move):
    return lax.ppermute(value, AXES, pairs(move))


def other_core(y, c, x, z):
    return (y, c + 1, x, z)


def first_axis(k):
    return lambda y, c, x, z: (y, c, x + k, z) if c == 0 else (y + k, c, x, z)


def second_axis(k):
    return lambda y, c, x, z: (y + k, c, x, z) if c == 0 else (y, c, x + k, z)


def along_y(k):
    return lambda y, c, x, z: (y + k, c, x, z)


def along_z(k):
    return lambda y, c, x, z: (y, c, x, z + k)


def f32(value):
    return value.astype(jnp.float32)


def shards(histories, lengths, cotangent, w_in):
    group, member = lax.axis_index("group"), lax.axis_index("member")
    y, core = group // 2, group % 2
    x, z = member // NZ, member % NZ
    first = jnp.where(core == 0, x, y)
    second = jnp.where(core == 0, y, x)
    where = jnp.stack([core, first, second, y]).astype(jnp.int32)
    theirs = permute(histories, other_core)
    keep, send = grads(where, lengths, histories, w_in, cotangent)
    recv = permute(send, other_core)
    xt = transposed(histories, theirs)
    parts = weights(where, xt, keep, recv)
    moved = [permute(parts[k], first_axis(k)) for k in (1, 2, 3)]
    grad_rows = row_grads(where, keep, send, w_in)
    summed = [f32(parts[0][l]) + f32(moved[0][l]) + f32(moved[1][l]) + f32(moved[2][l]) for l in range(4)]
    moved = [permute(summed[k].astype(jnp.bfloat16), second_axis(k)) for k in (1, 2, 3)]
    block = summed[0] + f32(moved[0]) + f32(moved[1]) + f32(moved[2])

    block = block.astype(jnp.bfloat16).reshape(NZ, 32, 256)
    nz = [[g * NZ + i for i in range(NZ)] for g in range(NX)]
    block = lax.all_to_all(block, "member", 0, 0, tiled=True, axis_index_groups=nz)
    block = jnp.sum(f32(block), axis=0)

    gathered = jnp.stack([block] + [permute(block, along_y(k)) for k in (1, 2, 3)])
    grad_w = place(where, gathered, permute(gathered, other_core))
    return (grad_rows, grad_w)


def solution(mesh):
    return jax.shard_map(
        shards,
        mesh=mesh,
        in_specs=(
            P(("group", "member"), None),
            P(("group", "member")),
            P(("group", "member"), None),
            P(),
        ),
        out_specs=(P(("group", "member"), None), P("member", None)),
        check_vma=False,
    )
```

```python
import jax
import jax.numpy as jnp
from jax import lax
from jax.sharding import PartitionSpec as P
from jax.experimental import pallas as pl
from jax.experimental.pallas import tpu as pltpu

HEADS = 4
BLOCK = 128
NT = (((1,), (1,)), ((), ()))
TN = (((0,), (0,)), ((), ()))


def mm(a, b, dims=(((1,), (0,)), ((), ()))):
    return lax.dot_general(a, b, dims, preferred_element_type=jnp.float32)


def grads_kernel(core_ref, len_ref, x_hbm, w_hbm, cot_hbm, keep_ref, send_ref,
                 x_ref, w_ref, cot_ref, slope_ref, act_ref, mask_ref, p_ref, s_ref, ds_ref,
                 att_ref, da_ref, g_ref, sems):
    rows, width = cot_ref.shape
    nblocks = rows // BLOCK
    size = width // HEADS
    half = width // 2
    scale = size ** -0.5
    bf16 = jnp.bfloat16

    def section(s):
        return pl.ds(s * width, width)

    loads = {s: pltpu.make_async_copy(w_hbm.at[:, section(s)], w_ref.at[:, section(s)], sems.at[s])
             for s in range(4)}
    load_x = pltpu.make_async_copy(x_hbm, x_ref, sems.at[4])
    load_cot = pltpu.make_async_copy(cot_hbm, cot_ref, sems.at[5])
    load_x.start()
    loads[2].start()
    loads[3].start()

    l0 = len_ref[0]
    l1 = len_ref[1]
    start1 = ((l0 + (BLOCK - 1)) // BLOCK) * BLOCK

    def spans(i):
        first = max(0, i - 2)
        return pl.ds(i * BLOCK, BLOCK), pl.ds(first * BLOCK, (i + 1 - first) * BLOCK), first

    def row_facts(i):
        row = i * BLOCK + lax.broadcasted_iota(jnp.int32, (BLOCK, 1), 0)
        in0 = row < l0
        in1 = (row >= start1) & (row < start1 + l1)
        return row, in0, in1

    for i in range(nblocks):
        r, keys, first = spans(i)
        row, in0, in1 = row_facts(i)
        low = jnp.where(in1, start1, 0)
        high = jnp.where(in0 | in1, row, -1)
        count = jnp.where(in0, l0, jnp.where(in1, l1, 1))
        inv = 1.0 / count.astype(jnp.float32)
        c = first * BLOCK + lax.broadcasted_iota(jnp.int32, (BLOCK, keys.size), 1)
        mask_ref[r, keys] = jnp.where((c >= low) & (c <= high), inv, 0.0)

    def project(s):
        loads[s].wait()
        h = mm(x_ref[...], w_ref[:, section(s)])
        sig = 0.5 * jnp.tanh(0.5 * h) + 0.5
        act = h * sig
        act_ref[:, section(s)] = act.astype(bf16)
        slope_ref[:, section(s)] = sig + act * (1.0 - sig)

    def col(s, h):
        return pl.ds(s * width + h * size, size)

    def head(h):
        return pl.ds(h * size, size)

    core = core_ref[0]

    def put(s, h, r, grad):
        value = grad.astype(bf16).astype(jnp.float32) * slope_ref[r, col(s, h)]
        to = s * half + (h % (HEADS // 2)) * size
        g_ref[(h // (HEADS // 2)) ^ core, r, pl.ds(to, size)] = value.astype(bf16)

    load_x.wait()
    loads[1].start()
    project(2)
    loads[0].start()
    load_cot.start()
    project(3)
    for i in range(nblocks):
        r, keys, _ = spans(i)
        for h in range(HEADS):
            t = mm(act_ref[r, col(2, h)], act_ref[keys, col(3, h)], NT) * scale
            sig = 0.5 * jnp.tanh(0.5 * t) + 0.5
            p = t * sig
            p_ref[h, r, keys] = (p * mask_ref[r, keys]).astype(bf16)
            s_ref[h, r, keys] = (sig + p * (1.0 - sig)) * mask_ref[r, keys]
    project(1)
    for i in range(nblocks):
        r, keys, _ = spans(i)
        for h in range(HEADS):
            att_ref[r, head(h)] = mm(p_ref[h, r, keys], act_ref[keys, col(1, h)])
    project(0)
    load_cot.wait()
    for i in range(nblocks):
        r, _, _ = spans(i)
        _, in0, in1 = row_facts(i)
        att = att_ref[r, :]
        cen = att - jnp.mean(att, axis=1, keepdims=True)
        rstd = lax.rsqrt(jnp.mean(cen * cen, axis=1, keepdims=True) + 1e-05)
        z = cen * rstd
        up = jnp.where(in0 | in1, cot_ref[r, :].astype(jnp.float32), 0.0)
        dz = up * act_ref[r, section(0)].astype(jnp.float32)
        m1 = jnp.mean(dz, axis=1, keepdims=True)
        m2 = jnp.mean(dz * z, axis=1, keepdims=True)
        da_ref[r, :] = ((dz - m1 - z * m2) * rstd).astype(bf16)
        du = up * z
        for h in range(HEADS):
            put(0, h, r, du[:, h * size:(h + 1) * size])
    for i in range(nblocks):
        r, keys, _ = spans(i)
        for h in range(HEADS):
            dp = mm(da_ref[r, head(h)], act_ref[keys, col(1, h)], NT)
            ds_ref[h, r, keys] = (dp * s_ref[h, r, keys]).astype(bf16)
    for i in range(nblocks):
        r, keys, _ = spans(i)
        for h in range(HEADS):
            put(2, h, r, mm(ds_ref[h, r, keys], act_ref[keys, col(3, h)]) * scale)
    for j in range(nblocks):
        last = min(nblocks, j + 3)
        r = pl.ds(j * BLOCK, BLOCK)
        qs = pl.ds(j * BLOCK, (last - j) * BLOCK)
        for h in range(HEADS):
            put(1, h, r, mm(p_ref[h, qs, r], da_ref[qs, head(h)], TN))
            put(3, h, r, mm(ds_ref[h, qs, r], act_ref[qs, col(2, h)], TN) * scale)
    keep_ref[...] = g_ref[0]
    send_ref[...] = g_ref[1]


def grads(core, lengths, x, w, cot):
    rows, d = x.shape
    width = cot.shape[1]
    wide = w.shape[1]
    vmem = pl.BlockSpec(memory_space=pltpu.VMEM)
    smem = pl.BlockSpec(memory_space=pltpu.SMEM)
    hbm = pl.BlockSpec(memory_space=pl.ANY)
    return pl.pallas_call(
        grads_kernel,
        out_shape=[jax.ShapeDtypeStruct((rows, wide // 2), jnp.bfloat16)] * 2,
        in_specs=[smem, smem, hbm, hbm, hbm],
        out_specs=[vmem, vmem],
        scratch_shapes=[
            pltpu.VMEM((rows, d), jnp.bfloat16),
            pltpu.VMEM((d, wide), jnp.bfloat16),
            pltpu.VMEM((rows, width), jnp.bfloat16),
            pltpu.VMEM((rows, wide), jnp.float32),
            pltpu.VMEM((rows, wide), jnp.bfloat16),
            pltpu.VMEM((rows, rows), jnp.float32),
            pltpu.VMEM((HEADS, rows, rows), jnp.bfloat16),
            pltpu.VMEM((HEADS, rows, rows), jnp.float32),
            pltpu.VMEM((HEADS, rows, rows), jnp.bfloat16),
            pltpu.VMEM((rows, width), jnp.float32),
            pltpu.VMEM((rows, width), jnp.bfloat16),
            pltpu.VMEM((2, rows, wide // 2), jnp.bfloat16),
            pltpu.SemaphoreType.DMA((6,)),
        ],
        compiler_params=pltpu.CompilerParams(vmem_limit_bytes=60 * 2**20),
        cost_estimate=pl.CostEstimate(flops=4 * 10**9, bytes_accessed=8 * 10**6, transcendentals=2 * 10**6),
        name="uvqk_grads",
    )(core, lengths, x, w, cot)


def transpose_kernel(x_ref, y_ref, xt_ref):
    rows, d = x_ref.shape
    for i, ref in enumerate((x_ref, y_ref)):
        for b in range(0, d, 256):
            for r in range(0, rows, 256):
                xt_ref[pl.ds(b, 256), pl.ds(i * rows + r, 256)] = ref[pl.ds(r, 256), pl.ds(b, 256)].T


def transposed(x, y):
    rows, d = x.shape
    vmem = pl.BlockSpec(memory_space=pltpu.VMEM)
    return pl.pallas_call(
        transpose_kernel,
        out_shape=jax.ShapeDtypeStruct((d, 2 * rows), jnp.bfloat16),
        in_specs=[vmem, vmem],
        out_specs=vmem,
        compiler_params=pltpu.CompilerParams(vmem_limit_bytes=16 * 2**20),
        cost_estimate=pl.CostEstimate(flops=0, bytes_accessed=4 * 2**20, transcendentals=0),
        name="transpose_rows",
    )(x, y)


def weights_kernel(where_ref, xt_ref, keep_ref, recv_ref, o0, o1, o2, o3):
    core, first, second = where_ref[0], where_ref[1], where_ref[2]
    rows = keep_ref.shape[0]
    for k, out in enumerate((o0, o1, o2, o3)):
        for l in range(4):
            a = lax.rem(first + k, 4)
            b = lax.rem(second + l, 4)
            rb = jnp.where(core == 0, a, b)
            cb = jnp.where(core == 0, b, a)
            rs = pl.ds(pl.multiple_of(rb * 256, 256), 256)
            cs = pl.ds(pl.multiple_of(cb * 256, 256), 256)
            total = mm(xt_ref[rs, pl.ds(0, rows)], keep_ref[:, cs])
            total += mm(xt_ref[rs, pl.ds(rows, rows)], recv_ref[:, cs])
            out[l] = total.astype(jnp.bfloat16)


def weights(where, xt, keep, recv):
    vmem = pl.BlockSpec(memory_space=pltpu.VMEM)
    smem = pl.BlockSpec(memory_space=pltpu.SMEM)
    return pl.pallas_call(
        weights_kernel,
        out_shape=[jax.ShapeDtypeStruct((4, 256, 256), jnp.bfloat16)] * 4,
        in_specs=[smem, vmem, vmem, vmem],
        out_specs=[vmem] * 4,
        compiler_params=pltpu.CompilerParams(vmem_limit_bytes=24 * 2**20),
        cost_estimate=pl.CostEstimate(flops=2 * 2**30, bytes_accessed=6 * 2**20, transcendentals=0),
        name="weight_grads",
    )(where, xt, keep, recv)


def rows_kernel(core_ref, keep_ref, send_ref, w_ref, out_ref):
    core = core_ref[0]
    rows = keep_ref.shape[0]
    for r in range(0, rows, 256):
        total = jnp.zeros((256, w_ref.shape[0]), jnp.float32)
        for i, ref in enumerate((keep_ref, send_ref)):
            for s in range(4):
                cols = pl.ds(pl.multiple_of(s * 512 + (core ^ i) * 256, 256), 256)
                total += mm(ref[pl.ds(r, 256), pl.ds(s * 256, 256)], w_ref[:, cols], NT)
        out_ref[pl.ds(r, 256), :] = total.astype(jnp.bfloat16)


def row_grads(core, keep, send, w):
    vmem = pl.BlockSpec(memory_space=pltpu.VMEM)
    smem = pl.BlockSpec(memory_space=pltpu.SMEM)
    return pl.pallas_call(
        rows_kernel,
        out_shape=jax.ShapeDtypeStruct((keep.shape[0], w.shape[0]), jnp.bfloat16),
        in_specs=[smem, vmem, vmem, vmem],
        out_specs=vmem,
        compiler_params=pltpu.CompilerParams(vmem_limit_bytes=24 * 2**20),
        cost_estimate=pl.CostEstimate(flops=2 * 2**30, bytes_accessed=7 * 2**20, transcendentals=0),
        name="row_grads",
    )(core, keep, send, w)


def place_kernel(where_ref, p0, p1, p2, p3, out_ref):
    core, y = where_ref[0], where_ref[3]
    for k, ref in enumerate((p0, p1, p2, p3)):
        s = lax.rem(y + 4 - k, 4)
        for i in range(2):
            cols = pl.ds(pl.multiple_of(s * 512 + (core ^ i) * 256, 256), 256)
            out_ref[:, cols] = ref[i]


def place(where, parts):
    vmem = pl.BlockSpec(memory_space=pltpu.VMEM)
    smem = pl.BlockSpec(memory_space=pltpu.SMEM)
    return pl.pallas_call(
        place_kernel,
        out_shape=jax.ShapeDtypeStruct((parts[0].shape[1], 2048), jnp.float32),
        in_specs=[smem] + [vmem] * 4,
        out_specs=vmem,
        compiler_params=pltpu.CompilerParams(vmem_limit_bytes=4 * 2**20),
        name="place_columns",
    )(where, *parts)


AXES = ("group", "member")
NY, NX, NZ = 4, 4, 8


def pairs(move):
    out = []
    for i in range(2 * NY * NX * NZ):
        g, m = divmod(i, NX * NZ)
        y, c = divmod(g, 2)
        x, z = divmod(m, NZ)
        y, c, x, z = move(y, c, x, z)
        out.append((i, ((y % NY) * 2 + c % 2) * NX * NZ + (x % NX) * NZ + z % NZ))
    return out


def permute(value, move):
    return lax.ppermute(value, AXES, pairs(move))


def other_core(y, c, x, z):
    return (y, c + 1, x, z)


def first_axis(k):
    return lambda y, c, x, z: (y, c, x + k, z) if c == 0 else (y + k, c, x, z)


def second_axis(k):
    return lambda y, c, x, z: (y + k, c, x, z) if c == 0 else (y, c, x + k, z)


def along_y(k):
    return lambda y, c, x, z: (y + k, c, x, z)


def along_z(k):
    return lambda y, c, x, z: (y, c, x, z + k)


def f32(value):
    return value.astype(jnp.float32)


def shards(histories, lengths, cotangent, w_in):
    group, member = lax.axis_index("group"), lax.axis_index("member")
    y, core = group // 2, group % 2
    x, z = member // NZ, member % NZ
    first = jnp.where(core == 0, x, y)
    second = jnp.where(core == 0, y, x)
    where = jnp.stack([core, first, second, y]).astype(jnp.int32)
    theirs = permute(histories, other_core)
    keep, send = grads(where, lengths, histories, w_in, cotangent)
    recv = permute(send, other_core)
    xt = transposed(histories, theirs)
    parts = weights(where, xt, keep, recv)
    moved = [permute(parts[k], first_axis(k)) for k in (1, 2, 3)]
    grad_rows = row_grads(where, keep, send, w_in)
    *moved, grad_rows = lax.optimization_barrier((*moved, grad_rows))
    summed = [f32(parts[0][l]) + f32(moved[0][l]) + f32(moved[1][l]) + f32(moved[2][l]) for l in range(4)]
    moved = [permute(summed[k].astype(jnp.bfloat16), second_axis(k)) for k in (1, 2, 3)]
    block = summed[0] + f32(moved[0]) + f32(moved[1]) + f32(moved[2])

    block = block.astype(jnp.bfloat16).reshape(NZ, 32, 256)
    nz = [[g * NZ + i for i in range(NZ)] for g in range(NX)]
    block = lax.all_to_all(block, "member", 0, 0, tiled=True, axis_index_groups=nz)
    block = jnp.sum(f32(block), axis=0)

    both = jnp.stack([block, permute(block, other_core)])
    grad_w = place(where, [both] + [permute(both, along_y(k)) for k in (1, 2, 3)])
    return (grad_rows, grad_w)


def solution(mesh):
    return jax.shard_map(
        shards,
        mesh=mesh,
        in_specs=(
            P(("group", "member"), None),
            P(("group", "member")),
            P(("group", "member"), None),
            P(),
        ),
        out_specs=(P(("group", "member"), None), P("member", None)),
        check_vma=False,
    )
```

```python
import jax
import jax.numpy as jnp
from jax import lax
from jax.sharding import PartitionSpec as P
from jax.experimental import pallas as pl
from jax.experimental.pallas import tpu as pltpu

HEADS = 4
BLOCK = 128
AXES = ("group", "member")
NY, NX, NZ = 4, 4, 8
NT = (((1,), (1,)), ((), ()))
TN = (((0,), (0,)), ((), ()))


def mm(a, b, dims=(((1,), (0,)), ((), ()))):
    return lax.dot_general(a, b, dims, preferred_element_type=jnp.float32)


def position():
    group, member = lax.axis_index("group"), lax.axis_index("member")
    return group // 2, group % 2, member // NZ, member % NZ


def grads_kernel(len_hbm, x_hbm, w_hbm, cot_hbm, keep_ref, send_ref,
                 len_ref, x_ref, w_ref, cot_ref, slope_ref, act_ref, mask_ref, p_ref, s_ref, ds_ref,
                 att_ref, da_ref, g_ref, sems):
    rows, width = cot_ref.shape
    nblocks = rows // BLOCK
    size = width // HEADS
    half = width // 2
    scale = size ** -0.5
    bf16 = jnp.bfloat16

    def section(s):
        return pl.ds(s * width, width)

    loads = {s: pltpu.make_async_copy(w_hbm.at[:, section(s)], w_ref.at[:, section(s)], sems.at[s])
             for s in range(4)}
    load_x = pltpu.make_async_copy(x_hbm, x_ref, sems.at[4])
    load_cot = pltpu.make_async_copy(cot_hbm, cot_ref, sems.at[5])
    load_len = pltpu.make_async_copy(len_hbm, len_ref, sems.at[6])
    load_len.start()
    load_x.start()
    loads[2].start()
    loads[3].start()
    load_len.wait()

    l0 = len_ref[0]
    l1 = len_ref[1]
    start1 = ((l0 + (BLOCK - 1)) // BLOCK) * BLOCK

    def spans(i):
        first = max(0, i - 2)
        return pl.ds(i * BLOCK, BLOCK), pl.ds(first * BLOCK, (i + 1 - first) * BLOCK), first

    def row_facts(i):
        row = i * BLOCK + lax.broadcasted_iota(jnp.int32, (BLOCK, 1), 0)
        in0 = row < l0
        in1 = (row >= start1) & (row < start1 + l1)
        return row, in0, in1

    for i in range(nblocks):
        r, keys, first = spans(i)
        row, in0, in1 = row_facts(i)
        low = jnp.where(in1, start1, 0)
        high = jnp.where(in0 | in1, row, -1)
        count = jnp.where(in0, l0, jnp.where(in1, l1, 1))
        inv = 1.0 / count.astype(jnp.float32)
        c = first * BLOCK + lax.broadcasted_iota(jnp.int32, (BLOCK, keys.size), 1)
        mask_ref[r, keys] = jnp.where((c >= low) & (c <= high), inv, 0.0)

    def project(s):
        loads[s].wait()
        h = mm(x_ref[...], w_ref[:, section(s)])
        sig = 0.5 * jnp.tanh(0.5 * h) + 0.5
        act = h * sig
        act_ref[:, section(s)] = act.astype(bf16)
        slope_ref[:, section(s)] = sig + act * (1.0 - sig)

    def col(s, h):
        return pl.ds(s * width + h * size, size)

    def head(h):
        return pl.ds(h * size, size)

    core = position()[1]

    def put(s, h, r, grad):
        value = grad.astype(bf16).astype(jnp.float32) * slope_ref[r, col(s, h)]
        to = s * half + (h % (HEADS // 2)) * size
        g_ref[(h // (HEADS // 2)) ^ core, r, pl.ds(to, size)] = value.astype(bf16)

    load_x.wait()
    loads[1].start()
    project(2)
    loads[0].start()
    load_cot.start()
    project(3)
    for i in range(nblocks):
        r, keys, _ = spans(i)
        for h in range(HEADS):
            t = mm(act_ref[r, col(2, h)], act_ref[keys, col(3, h)], NT) * scale
            sig = 0.5 * jnp.tanh(0.5 * t) + 0.5
            p = t * sig
            p_ref[h, r, keys] = (p * mask_ref[r, keys]).astype(bf16)
            s_ref[h, r, keys] = (sig + p * (1.0 - sig)) * mask_ref[r, keys]
    project(1)
    for i in range(nblocks):
        r, keys, _ = spans(i)
        for h in range(HEADS):
            att_ref[r, head(h)] = mm(p_ref[h, r, keys], act_ref[keys, col(1, h)])
    project(0)
    load_cot.wait()
    for i in range(nblocks):
        r, _, _ = spans(i)
        _, in0, in1 = row_facts(i)
        att = att_ref[r, :]
        cen = att - jnp.mean(att, axis=1, keepdims=True)
        rstd = lax.rsqrt(jnp.mean(cen * cen, axis=1, keepdims=True) + 1e-05)
        z = cen * rstd
        up = jnp.where(in0 | in1, cot_ref[r, :].astype(jnp.float32), 0.0)
        dz = up * act_ref[r, section(0)].astype(jnp.float32)
        m1 = jnp.mean(dz, axis=1, keepdims=True)
        m2 = jnp.mean(dz * z, axis=1, keepdims=True)
        da_ref[r, :] = ((dz - m1 - z * m2) * rstd).astype(bf16)
        du = up * z
        for h in range(HEADS):
            put(0, h, r, du[:, h * size:(h + 1) * size])
    for i in range(nblocks):
        r, keys, _ = spans(i)
        for h in range(HEADS):
            dp = mm(da_ref[r, head(h)], act_ref[keys, col(1, h)], NT)
            ds_ref[h, r, keys] = (dp * s_ref[h, r, keys]).astype(bf16)
    for i in range(nblocks):
        r, keys, _ = spans(i)
        for h in range(HEADS):
            put(2, h, r, mm(ds_ref[h, r, keys], act_ref[keys, col(3, h)]) * scale)
    for j in range(nblocks):
        last = min(nblocks, j + 3)
        r = pl.ds(j * BLOCK, BLOCK)
        qs = pl.ds(j * BLOCK, (last - j) * BLOCK)
        for h in range(HEADS):
            put(1, h, r, mm(p_ref[h, qs, r], da_ref[qs, head(h)], TN))
            put(3, h, r, mm(ds_ref[h, qs, r], act_ref[qs, col(2, h)], TN) * scale)
    keep_ref[...] = g_ref[0]
    send_ref[...] = g_ref[1]


def grads(lengths, x, w, cot):
    rows, d = x.shape
    width = cot.shape[1]
    wide = w.shape[1]
    vmem = pl.BlockSpec(memory_space=pltpu.VMEM)
    hbm = pl.BlockSpec(memory_space=pl.ANY)
    return pl.pallas_call(
        grads_kernel,
        out_shape=[pltpu.VMEM((rows, wide // 2), jnp.bfloat16)] * 2,
        in_specs=[hbm] * 4,
        out_specs=[vmem, vmem],
        scratch_shapes=[
            pltpu.SMEM((2,), jnp.int32),
            pltpu.VMEM((rows, d), jnp.bfloat16),
            pltpu.VMEM((d, wide), jnp.bfloat16),
            pltpu.VMEM((rows, width), jnp.bfloat16),
            pltpu.VMEM((rows, wide), jnp.float32),
            pltpu.VMEM((rows, wide), jnp.bfloat16),
            pltpu.VMEM((rows, rows), jnp.float32),
            pltpu.VMEM((HEADS, rows, rows), jnp.bfloat16),
            pltpu.VMEM((HEADS, rows, rows), jnp.float32),
            pltpu.VMEM((HEADS, rows, rows), jnp.bfloat16),
            pltpu.VMEM((rows, width), jnp.float32),
            pltpu.VMEM((rows, width), jnp.bfloat16),
            pltpu.VMEM((2, rows, wide // 2), jnp.bfloat16),
            pltpu.SemaphoreType.DMA((7,)),
        ],
        compiler_params=pltpu.CompilerParams(vmem_limit_bytes=40 * 2**20),
        cost_estimate=pl.CostEstimate(flops=4 * 10**9, bytes_accessed=8 * 10**6, transcendentals=2 * 10**6),
        name="uvqk_grads",
    )(*[pltpu.with_memory_space_constraint(v, pltpu.HBM) for v in (lengths, x, w, cot)])


def flip(ref, out_ref):
    rows, d = ref.shape
    z = position()[3]
    for b in range(0, d, 256):
        for r in range(0, rows, 256):
            block = ref[pl.ds(r, 256), pl.ds(b, 256)].T
            for j in range(NZ):
                at = pl.multiple_of(b + (j ^ z) * 32, 32)
                out_ref[pl.ds(at, 32), pl.ds(r, 256)] = block[j * 32:(j + 1) * 32]


def blocks_of():
    y, core, x, _ = position()
    first = jnp.where(core == 0, x, y)
    second = jnp.where(core == 0, y, x)
    for k in range(4):
        for l in range(4):
            a = first ^ k
            b = second ^ l
            rb = jnp.where(core == 0, a, b)
            cb = jnp.where(core == 0, b, a)
            yield k, l, pl.ds(pl.multiple_of(rb * 256, 256), 256), pl.ds(pl.multiple_of(cb * 256, 256), 256)


def own_kernel(x_ref, theirs_ref, keep_ref, acc_ref, xt_ref, own_ref):
    flip(x_ref, own_ref)
    for k, l, rs, cs in blocks_of():
        acc_ref[k, l] = mm(own_ref[rs, :], keep_ref[:, cs])
    flip(theirs_ref, xt_ref)


def own_part(x, theirs, keep):
    rows, d = x.shape
    vmem = pl.BlockSpec(memory_space=pltpu.VMEM)
    return pl.pallas_call(
        own_kernel,
        out_shape=[jax.ShapeDtypeStruct((4, 4, 256, 256), jnp.float32), jax.ShapeDtypeStruct((d, rows), jnp.bfloat16)],
        in_specs=[vmem] * 3,
        out_specs=[vmem, vmem],
        scratch_shapes=[pltpu.VMEM((d, rows), jnp.bfloat16)],
        compiler_params=pltpu.CompilerParams(vmem_limit_bytes=24 * 2**20),
        cost_estimate=pl.CostEstimate(flops=2**30, bytes_accessed=6 * 2**20, transcendentals=0),
        name="own_weight_grads",
    )(x, theirs, keep)


def pair_kernel(acc_ref, xt_ref, recv_ref, o0, o1, o2, o3):
    outs = (o0, o1, o2, o3)
    for k, l, rs, cs in blocks_of():
        outs[k][l] = (acc_ref[k, l] + mm(xt_ref[rs, :], recv_ref[:, cs])).astype(jnp.bfloat16)


def pair_part(acc, xt, recv):
    vmem = pl.BlockSpec(memory_space=pltpu.VMEM)
    return pl.pallas_call(
        pair_kernel,
        out_shape=[jax.ShapeDtypeStruct((4, 256, 256), jnp.bfloat16)] * 4,
        in_specs=[vmem] * 3,
        out_specs=[vmem] * 4,
        compiler_params=pltpu.CompilerParams(vmem_limit_bytes=24 * 2**20),
        cost_estimate=pl.CostEstimate(flops=2**30, bytes_accessed=6 * 2**20, transcendentals=0),
        name="pair_weight_grads",
    )(acc, xt, recv)


def rows_kernel(keep_ref, send_ref, w_ref, out_ref):
    core = position()[1]
    rows = keep_ref.shape[0]
    for r in range(0, rows, 256):
        total = jnp.zeros((256, w_ref.shape[0]), jnp.float32)
        for i, ref in enumerate((keep_ref, send_ref)):
            for s in range(4):
                cols = pl.ds(pl.multiple_of(s * 512 + (core ^ i) * 256, 256), 256)
                total += mm(ref[pl.ds(r, 256), pl.ds(s * 256, 256)], w_ref[:, cols], NT)
        out_ref[pl.ds(r, 256), :] = total.astype(jnp.bfloat16)


def row_grads(keep, send, w):
    vmem = pl.BlockSpec(memory_space=pltpu.VMEM)
    return pl.pallas_call(
        rows_kernel,
        out_shape=jax.ShapeDtypeStruct((keep.shape[0], w.shape[0]), jnp.bfloat16),
        in_specs=[vmem] * 3,
        out_specs=vmem,
        compiler_params=pltpu.CompilerParams(vmem_limit_bytes=24 * 2**20),
        cost_estimate=pl.CostEstimate(flops=2 * 2**30, bytes_accessed=7 * 2**20, transcendentals=0),
        name="row_grads",
    )(keep, send, w)


def place_kernel(p0, p1, p2, p3, out_ref):
    y, core, _, _ = position()
    for k, ref in enumerate((p0, p1, p2, p3)):
        s = y ^ k
        for i in range(2):
            cols = pl.ds(pl.multiple_of(s * 512 + (core ^ i) * 256, 256), 256)
            out_ref[:, cols] = ref[i]


def place(parts):
    vmem = pl.BlockSpec(memory_space=pltpu.VMEM)
    return pl.pallas_call(
        place_kernel,
        out_shape=jax.ShapeDtypeStruct((parts[0].shape[1], 2048), jnp.float32),
        in_specs=[vmem] * 4,
        out_specs=vmem,
        compiler_params=pltpu.CompilerParams(vmem_limit_bytes=4 * 2**20),
        name="place_columns",
    )(*parts)


def pairs(move):
    out = []
    for i in range(2 * NY * NX * NZ):
        g, m = divmod(i, NX * NZ)
        y, c = divmod(g, 2)
        x, z = divmod(m, NZ)
        y, c, x, z = move(y, c, x, z)
        out.append((i, ((y % NY) * 2 + c % 2) * NX * NZ + (x % NX) * NZ + z % NZ))
    return out


def permute(value, move):
    return lax.ppermute(value, AXES, pairs(move))


def other_core(y, c, x, z):
    return (y, c + 1, x, z)


def first_axis(k):
    return lambda y, c, x, z: (y, c, x ^ k, z) if c == 0 else (y ^ k, c, x, z)


def second_axis(k):
    return lambda y, c, x, z: (y ^ k, c, x, z) if c == 0 else (y, c, x ^ k, z)


def along_y(k):
    return lambda y, c, x, z: (y ^ k, c, x, z)


def along_z(k):
    return lambda y, c, x, z: (y, c, x, z ^ k)


def f32(value):
    return value.astype(jnp.float32)


def shards(histories, lengths, cotangent, w_in):
    theirs = permute(histories, other_core)
    keep, send = grads(lengths, histories, w_in, cotangent)
    recv = permute(send, other_core)
    acc, xt = own_part(histories, theirs, keep)
    parts = pair_part(acc, xt, recv)
    moved = [permute(parts[k], first_axis(k)) for k in (1, 3, 2)]
    grad_rows = row_grads(keep, send, w_in)
    *moved, grad_rows = lax.optimization_barrier((*moved, grad_rows))
    summed = [f32(parts[0][l]) + f32(moved[0][l]) + f32(moved[1][l]) + f32(moved[2][l]) for l in range(4)]
    moved = [permute(summed[k].astype(jnp.bfloat16), second_axis(k)) for k in (1, 2, 3)]
    block = summed[0] + f32(moved[0]) + f32(moved[1]) + f32(moved[2])
    block = block.reshape(NZ, 32, 256)
    ends = jnp.stack([block[0], block[7]])
    moved = [permute(jnp.stack([block[m], block[7 - m]]).astype(jnp.bfloat16), along_z(m)) for m in (1, 2, 3)]
    ends = ends + f32(moved[0]) + f32(moved[1]) + f32(moved[2])
    block = ends[0] + permute(ends[1], along_z(7))

    both = jnp.stack([block, permute(block, other_core)])
    grad_w = place([both] + [permute(both, along_y(k)) for k in (1, 2, 3)])
    return (grad_rows, grad_w)


def solution(mesh):
    return jax.shard_map(
        shards,
        mesh=mesh,
        in_specs=(
            P(("group", "member"), None),
            P(("group", "member")),
            P(("group", "member"), None),
            P(),
        ),
        out_specs=(P(("group", "member"), None), P("member", None)),
        check_vma=False,
    )
```

```python
import functools

import jax
import jax.numpy as jnp
from jax import lax
from jax.sharding import PartitionSpec as P
from jax.experimental import pallas as pl
from jax.experimental.pallas import tpu as pltpu

HEADS = 4
BLOCK = 128
AXES = ("group", "member")
NY, NX, NZ = 4, 4, 8
NT = (((1,), (1,)), ((), ()))
TN = (((0,), (0,)), ((), ()))


def mm(a, b, dims=(((1,), (0,)), ((), ()))):
    return lax.dot_general(a, b, dims, preferred_element_type=jnp.float32)


def position():
    group, member = lax.axis_index("group"), lax.axis_index("member")
    return group // 2, group % 2, member // NZ, member % NZ


def grads_kernel(len_hbm, x_hbm, w_hbm, cot_hbm, keep_ref, send_ref,
                 len_ref, x_ref, w_ref, cot_ref, slope_ref, act_ref, mask_ref, p_ref, s_ref, ds_ref,
                 att_ref, da_ref, g_ref, sems):
    rows, width = cot_ref.shape
    nblocks = rows // BLOCK
    size = width // HEADS
    half = width // 2
    scale = size ** -0.5
    bf16 = jnp.bfloat16

    def section(s):
        return pl.ds(s * width, width)

    loads = {s: pltpu.make_async_copy(w_hbm.at[:, section(s)], w_ref.at[:, section(s)], sems.at[s])
             for s in range(4)}
    load_x = pltpu.make_async_copy(x_hbm, x_ref, sems.at[4])
    load_cot = pltpu.make_async_copy(cot_hbm, cot_ref, sems.at[5])
    load_len = pltpu.make_async_copy(len_hbm, len_ref, sems.at[6])
    load_len.start()
    load_x.start()
    loads[2].start()
    loads[3].start()
    load_len.wait()

    l0 = len_ref[0]
    l1 = len_ref[1]
    start1 = ((l0 + (BLOCK - 1)) // BLOCK) * BLOCK

    def spans(i):
        first = max(0, i - 2)
        return pl.ds(i * BLOCK, BLOCK), pl.ds(first * BLOCK, (i + 1 - first) * BLOCK), first

    def row_facts(i):
        row = i * BLOCK + lax.broadcasted_iota(jnp.int32, (BLOCK, 1), 0)
        in0 = row < l0
        in1 = (row >= start1) & (row < start1 + l1)
        return row, in0, in1

    for i in range(nblocks):
        r, keys, first = spans(i)
        row, in0, in1 = row_facts(i)
        low = jnp.where(in1, start1, 0)
        high = jnp.where(in0 | in1, row, -1)
        count = jnp.where(in0, l0, jnp.where(in1, l1, 1))
        inv = 1.0 / count.astype(jnp.float32)
        c = first * BLOCK + lax.broadcasted_iota(jnp.int32, (BLOCK, keys.size), 1)
        mask_ref[r, keys] = jnp.where((c >= low) & (c <= high), inv, 0.0)

    def project(s):
        loads[s].wait()
        h = mm(x_ref[...], w_ref[:, section(s)])
        sig = 0.5 * jnp.tanh(0.5 * h) + 0.5
        act = h * sig
        act_ref[:, section(s)] = act.astype(bf16)
        slope_ref[:, section(s)] = sig + act * (1.0 - sig)

    def col(s, h):
        return pl.ds(s * width + h * size, size)

    def head(h):
        return pl.ds(h * size, size)

    core = position()[1]

    def put(s, h, r, grad):
        value = grad.astype(bf16).astype(jnp.float32) * slope_ref[r, col(s, h)]
        to = s * half + (h % (HEADS // 2)) * size
        g_ref[(h // (HEADS // 2)) ^ core, r, pl.ds(to, size)] = value.astype(bf16)

    load_x.wait()
    loads[1].start()
    project(2)
    loads[0].start()
    load_cot.start()
    project(3)
    for i in range(nblocks):
        r, keys, _ = spans(i)
        for h in range(HEADS):
            t = mm(act_ref[r, col(2, h)], act_ref[keys, col(3, h)], NT) * scale
            sig = 0.5 * jnp.tanh(0.5 * t) + 0.5
            p = t * sig
            p_ref[h, r, keys] = (p * mask_ref[r, keys]).astype(bf16)
            s_ref[h, r, keys] = (sig + p * (1.0 - sig)) * mask_ref[r, keys]
    project(1)
    project(0)
    load_cot.wait()
    for i in range(nblocks):
        r, keys, _ = spans(i)
        for h in range(HEADS):
            att_ref[r, head(h)] = mm(p_ref[h, r, keys], act_ref[keys, col(1, h)])
        _, in0, in1 = row_facts(i)
        att = att_ref[r, :]
        cen = att - jnp.mean(att, axis=1, keepdims=True)
        rstd = lax.rsqrt(jnp.mean(cen * cen, axis=1, keepdims=True) + 1e-05)
        z = cen * rstd
        up = jnp.where(in0 | in1, cot_ref[r, :].astype(jnp.float32), 0.0)
        dz = up * act_ref[r, section(0)].astype(jnp.float32)
        m1 = jnp.mean(dz, axis=1, keepdims=True)
        m2 = jnp.mean(dz * z, axis=1, keepdims=True)
        da_ref[r, :] = ((dz - m1 - z * m2) * rstd).astype(bf16)
        du = up * z
        for h in range(HEADS):
            put(0, h, r, du[:, h * size:(h + 1) * size])
    for i in range(nblocks):
        r, keys, _ = spans(i)
        for h in range(HEADS):
            dp = mm(da_ref[r, head(h)], act_ref[keys, col(1, h)], NT)
            ds_ref[h, r, keys] = (dp * s_ref[h, r, keys]).astype(bf16)
    for i in range(nblocks):
        r, keys, _ = spans(i)
        for h in range(HEADS):
            put(2, h, r, mm(ds_ref[h, r, keys], act_ref[keys, col(3, h)]) * scale)
    for j in range(nblocks):
        last = min(nblocks, j + 3)
        r = pl.ds(j * BLOCK, BLOCK)
        qs = pl.ds(j * BLOCK, (last - j) * BLOCK)
        for h in range(HEADS):
            put(1, h, r, mm(p_ref[h, qs, r], da_ref[qs, head(h)], TN))
            put(3, h, r, mm(ds_ref[h, qs, r], act_ref[qs, col(2, h)], TN) * scale)
    keep_ref[...] = g_ref[0]
    send_ref[...] = g_ref[1]


def grads(lengths, x, w, cot):
    rows, d = x.shape
    width = cot.shape[1]
    wide = w.shape[1]
    vmem = pl.BlockSpec(memory_space=pltpu.VMEM)
    hbm = pl.BlockSpec(memory_space=pl.ANY)
    return pl.pallas_call(
        grads_kernel,
        out_shape=[pltpu.VMEM((rows, wide // 2), jnp.bfloat16)] * 2,
        in_specs=[hbm] * 4,
        out_specs=[vmem, vmem],
        scratch_shapes=[
            pltpu.SMEM((2,), jnp.int32),
            pltpu.VMEM((rows, d), jnp.bfloat16),
            pltpu.VMEM((d, wide), jnp.bfloat16),
            pltpu.VMEM((rows, width), jnp.bfloat16),
            pltpu.VMEM((rows, wide), jnp.float32),
            pltpu.VMEM((rows, wide), jnp.bfloat16),
            pltpu.VMEM((rows, rows), jnp.float32),
            pltpu.VMEM((HEADS, rows, rows), jnp.bfloat16),
            pltpu.VMEM((HEADS, rows, rows), jnp.float32),
            pltpu.VMEM((HEADS, rows, rows), jnp.bfloat16),
            pltpu.VMEM((rows, width), jnp.float32),
            pltpu.VMEM((rows, width), jnp.bfloat16),
            pltpu.VMEM((2, rows, wide // 2), jnp.bfloat16),
            pltpu.SemaphoreType.DMA((7,)),
        ],
        compiler_params=pltpu.CompilerParams(vmem_limit_bytes=40 * 2**20),
        cost_estimate=pl.CostEstimate(flops=4 * 10**9, bytes_accessed=8 * 10**6, transcendentals=2 * 10**6),
        name="uvqk_grads",
    )(*[pltpu.with_memory_space_constraint(v, pltpu.HBM) for v in (lengths, x, w, cot)])


def flip(ref, out_ref):
    rows, d = ref.shape
    z = position()[3]
    for b in range(0, d, 256):
        for r in range(0, rows, 256):
            block = ref[pl.ds(r, 256), pl.ds(b, 256)].T
            for j in range(NZ):
                at = pl.multiple_of(b + (j ^ z) * 32, 32)
                out_ref[pl.ds(at, 32), pl.ds(r, 256)] = block[j * 32:(j + 1) * 32]


def blocks_of():
    y, core, x, _ = position()
    first = jnp.where(core == 0, x, y)
    second = jnp.where(core == 0, y, x)
    for k in range(4):
        for l in range(4):
            a = first ^ k
            b = second ^ l
            rb = jnp.where(core == 0, a, b)
            cb = jnp.where(core == 0, b, a)
            yield k, l, pl.ds(pl.multiple_of(rb * 256, 256), 256), pl.ds(pl.multiple_of(cb * 256, 256), 256)


def own_kernel(x_ref, theirs_ref, keep_ref, a0, a1, a2, a3, xt_ref, own_ref):
    flip(x_ref, own_ref)
    sums = (a0, a1, a2, a3)
    for k, l, rs, cs in blocks_of():
        sums[k][l] = mm(own_ref[rs, :], keep_ref[:, cs])
    flip(theirs_ref, xt_ref)


def own_part(x, theirs, keep):
    rows, d = x.shape
    vmem = pl.BlockSpec(memory_space=pltpu.VMEM)
    return pl.pallas_call(
        own_kernel,
        out_shape=[pltpu.VMEM((4, 256, 256), jnp.float32)] * 4 + [pltpu.VMEM((d, rows), jnp.bfloat16)],
        in_specs=[vmem] * 3,
        out_specs=[vmem] * 5,
        scratch_shapes=[pltpu.VMEM((d, rows), jnp.bfloat16)],
        compiler_params=pltpu.CompilerParams(vmem_limit_bytes=24 * 2**20),
        cost_estimate=pl.CostEstimate(flops=2**30, bytes_accessed=6 * 2**20, transcendentals=0),
        name="own_weight_grads",
    )(x, theirs, keep)


def pair_kernel(ks, *refs):
    n = len(ks)
    xt_ref, recv_ref = refs[n:n + 2]
    for k, l, rs, cs in blocks_of():
        if k in ks:
            at = ks.index(k)
            total = refs[at][l] + mm(xt_ref[rs, :], recv_ref[:, cs])
            refs[n + 2 + at][l] = total.astype(jnp.bfloat16)


def pair_part(ks, sums, xt, recv):
    vmem = pl.BlockSpec(memory_space=pltpu.VMEM)
    n = len(ks)
    return pl.pallas_call(
        functools.partial(pair_kernel, ks),
        out_shape=[pltpu.VMEM((4, 256, 256), jnp.bfloat16)] * n,
        in_specs=[vmem] * (n + 2),
        out_specs=[vmem] * n,
        compiler_params=pltpu.CompilerParams(vmem_limit_bytes=24 * 2**20),
        cost_estimate=pl.CostEstimate(flops=n * 2**28, bytes_accessed=(2 * n + 2) * 2**20, transcendentals=0),
        name="pair_weight_grads",
    )(*[sums[k] for k in ks], xt, recv)


def rows_kernel(keep_ref, send_ref, w_ref, out_ref):
    core = position()[1]
    rows = keep_ref.shape[0]
    for r in range(0, rows, 256):
        total = jnp.zeros((256, w_ref.shape[0]), jnp.float32)
        for i, ref in enumerate((keep_ref, send_ref)):
            for s in range(4):
                cols = pl.ds(pl.multiple_of(s * 512 + (core ^ i) * 256, 256), 256)
                total += mm(ref[pl.ds(r, 256), pl.ds(s * 256, 256)], w_ref[:, cols], NT)
        out_ref[pl.ds(r, 256), :] = total.astype(jnp.bfloat16)


def row_grads(keep, send, w):
    vmem = pl.BlockSpec(memory_space=pltpu.VMEM)
    return pl.pallas_call(
        rows_kernel,
        out_shape=jax.ShapeDtypeStruct((keep.shape[0], w.shape[0]), jnp.bfloat16),
        in_specs=[vmem] * 3,
        out_specs=vmem,
        compiler_params=pltpu.CompilerParams(vmem_limit_bytes=24 * 2**20),
        cost_estimate=pl.CostEstimate(flops=2 * 2**30, bytes_accessed=7 * 2**20, transcendentals=0),
        name="row_grads",
    )(keep, send, w)


def place_kernel(p0, p1, p2, p3, out_ref):
    y, core, _, _ = position()
    for k, ref in enumerate((p0, p1, p2, p3)):
        s = y ^ k
        for i in range(2):
            cols = pl.ds(pl.multiple_of(s * 512 + (core ^ i) * 256, 256), 256)
            out_ref[:, cols] = ref[i].astype(jnp.float32)


def place(parts):
    vmem = pl.BlockSpec(memory_space=pltpu.VMEM)
    return pl.pallas_call(
        place_kernel,
        out_shape=jax.ShapeDtypeStruct((parts[0].shape[1], 2048), jnp.float32),
        in_specs=[vmem] * 4,
        out_specs=vmem,
        compiler_params=pltpu.CompilerParams(vmem_limit_bytes=4 * 2**20),
        name="place_columns",
    )(*parts)


def pairs(move):
    out = []
    for i in range(2 * NY * NX * NZ):
        g, m = divmod(i, NX * NZ)
        y, c = divmod(g, 2)
        x, z = divmod(m, NZ)
        y, c, x, z = move(y, c, x, z)
        out.append((i, ((y % NY) * 2 + c % 2) * NX * NZ + (x % NX) * NZ + z % NZ))
    return out


def permute(value, move):
    return lax.ppermute(value, AXES, pairs(move))


def other_core(y, c, x, z):
    return (y, c + 1, x, z)


def first_axis(k):
    return lambda y, c, x, z: (y, c, x ^ k, z) if c == 0 else (y ^ k, c, x, z)


def second_axis(k):
    return lambda y, c, x, z: (y ^ k, c, x, z) if c == 0 else (y, c, x ^ k, z)


def along_y(k):
    return lambda y, c, x, z: (y ^ k, c, x, z)


def along_z(k):
    return lambda y, c, x, z: (y, c, x, z ^ k)


def f32(value):
    return value.astype(jnp.float32)


def shards(histories, lengths, cotangent, w_in):
    theirs = permute(histories, other_core)
    keep, send = grads(lengths, histories, w_in, cotangent)
    recv = permute(send, other_core)
    *sums, xt = own_part(histories, theirs, keep)
    far, = pair_part((2,), sums, xt, recv)
    near, last = pair_part((1, 3), sums, xt, recv)
    moved = [permute(part, first_axis(k)) for k, part in ((2, far), (1, near), (3, last))]
    mine, = pair_part((0,), sums, xt, recv)
    grad_rows = row_grads(keep, send, w_in)
    *moved, mine, grad_rows = lax.optimization_barrier((*moved, mine, grad_rows))
    summed = [f32(mine[l]) + f32(moved[0][l]) + f32(moved[1][l]) + f32(moved[2][l]) for l in range(4)]
    moved = [permute(summed[k].astype(jnp.bfloat16), second_axis(k)) for k in (1, 3, 2)]
    block = summed[0] + f32(moved[0]) + f32(moved[1]) + f32(moved[2])
    block = block.reshape(NZ, 32, 256)
    ends = jnp.stack([block[0], block[7]])
    moved = [permute(jnp.stack([block[m], block[7 - m]]).astype(jnp.bfloat16), along_z(m)) for m in (1, 2, 3)]
    ends = ends + f32(moved[0]) + f32(moved[1]) + f32(moved[2])
    block = ends[0] + permute(ends[1], along_z(7))

    block = block.astype(jnp.bfloat16)
    both = jnp.stack([block, permute(block, other_core)])
    gathered = {k: permute(both, along_y(k)) for k in (2, 1, 3)}
    grad_w = place([both, gathered[1], gathered[2], gathered[3]])
    return (grad_rows, grad_w)


def solution(mesh):
    return jax.shard_map(
        shards,
        mesh=mesh,
        in_specs=(
            P(("group", "member"), None),
            P(("group", "member")),
            P(("group", "member"), None),
            P(),
        ),
        out_specs=(P(("group", "member"), None), P("member", None)),
        check_vma=False,
    )
```

```python
import functools

import jax
import jax.numpy as jnp
from jax import lax
from jax.sharding import PartitionSpec as P
from jax.experimental import pallas as pl
from jax.experimental.pallas import tpu as pltpu

HEADS = 4
BLOCK = 128
AXES = ("group", "member")
NY, NX, NZ = 4, 4, 8
NT = (((1,), (1,)), ((), ()))
TN = (((0,), (0,)), ((), ()))


def mm(a, b, dims=(((1,), (0,)), ((), ()))):
    return lax.dot_general(a, b, dims, preferred_element_type=jnp.float32)


def position():
    group, member = lax.axis_index("group"), lax.axis_index("member")
    return group // 2, group % 2, member // NZ, member % NZ


def spans(i):
    first = max(0, i - 2)
    return pl.ds(i * BLOCK, BLOCK), pl.ds(first * BLOCK, (i + 1 - first) * BLOCK), first


def col(s, h):
    return pl.ds(pl.multiple_of((s * HEADS + h) * BLOCK, BLOCK), BLOCK)


def head(h):
    return col(0, h)


def store(s, j, out_ref, h, r, slope_ref, grad):
    if s == 0:
        grad = grad[r, head(h)]
    value = grad.astype(jnp.bfloat16).astype(jnp.float32) * slope_ref[r, col(s, h)]
    out_ref[r, pl.ds((s * (HEADS // 2) + j) * BLOCK, BLOCK)] = value.astype(jnp.bfloat16)


def backward(side, out_ref, slope_ref, act_ref, p_ref, s_ref, ds_ref, da_ref):
    nblocks = act_ref.shape[0] // BLOCK
    scale = BLOCK ** -0.5
    heads = [(j, side * (HEADS // 2) + j) for j in range(HEADS // 2)]
    for i in range(nblocks):
        r, keys, _ = spans(i)
        for j, h in heads:
            dp = mm(da_ref[r, head(h)], act_ref[keys, col(1, h)], NT)
            ds_ref[j, r, keys] = (dp * s_ref[h, r, keys]).astype(jnp.bfloat16)
    for i in range(nblocks):
        r, keys, _ = spans(i)
        for j, h in heads:
            dq = mm(ds_ref[j, r, keys], act_ref[keys, col(3, h)]) * scale
            store(2, j, out_ref, h, r, slope_ref, dq)
    for b in range(nblocks):
        last = min(nblocks, b + 3)
        r = pl.ds(b * BLOCK, BLOCK)
        qs = pl.ds(b * BLOCK, (last - b) * BLOCK)
        for j, h in heads:
            dv = mm(p_ref[h, qs, r], da_ref[qs, head(h)], TN)
            store(1, j, out_ref, h, r, slope_ref, dv)
            dk = mm(ds_ref[j, qs, r], act_ref[qs, col(2, h)], TN) * scale
            store(3, j, out_ref, h, r, slope_ref, dk)


def grads_kernel(len_hbm, x_hbm, w_hbm, cot_hbm, send_ref, keep_u_ref, slope_ref, act_ref, p_ref, s_ref, da_ref,
                 len_ref, x_ref, w_ref, cot_ref, mask_ref, ds_ref, att_ref, sems):
    rows, width = cot_ref.shape
    nblocks = rows // BLOCK
    size = width // HEADS
    half = width // 2
    scale = size ** -0.5
    bf16 = jnp.bfloat16

    def section(s):
        return pl.ds(s * width, width)

    loads = {s: pltpu.make_async_copy(w_hbm.at[:, section(s)], w_ref.at[:, section(s)], sems.at[s])
             for s in range(4)}
    load_x = pltpu.make_async_copy(x_hbm, x_ref, sems.at[4])
    load_cot = pltpu.make_async_copy(cot_hbm, cot_ref, sems.at[5])
    load_len = pltpu.make_async_copy(len_hbm, len_ref, sems.at[6])
    load_len.start()
    load_x.start()
    loads[2].start()
    loads[3].start()
    load_len.wait()

    l0 = len_ref[0]
    l1 = len_ref[1]
    start1 = ((l0 + (BLOCK - 1)) // BLOCK) * BLOCK

    def row_facts(i):
        row = i * BLOCK + lax.broadcasted_iota(jnp.int32, (BLOCK, 1), 0)
        in0 = row < l0
        in1 = (row >= start1) & (row < start1 + l1)
        return row, in0, in1

    for i in range(nblocks):
        r, keys, first = spans(i)
        row, in0, in1 = row_facts(i)
        low = jnp.where(in1, start1, 0)
        high = jnp.where(in0 | in1, row, -1)
        count = jnp.where(in0, l0, jnp.where(in1, l1, 1))
        inv = 1.0 / count.astype(jnp.float32)
        c = first * BLOCK + lax.broadcasted_iota(jnp.int32, (BLOCK, keys.size), 1)
        mask_ref[r, keys] = jnp.where((c >= low) & (c <= high), inv, 0.0)

    def project(s):
        loads[s].wait()
        h = mm(x_ref[...], w_ref[:, section(s)])
        sig = 0.5 * jnp.tanh(0.5 * h) + 0.5
        act = h * sig
        act_ref[:, section(s)] = act.astype(bf16)
        slope_ref[:, section(s)] = sig + act * (1.0 - sig)

    core = position()[1]

    load_x.wait()
    loads[1].start()
    project(2)
    loads[0].start()
    load_cot.start()
    project(3)
    for i in range(nblocks):
        r, keys, _ = spans(i)
        for h in range(HEADS):
            t = mm(act_ref[r, col(2, h)], act_ref[keys, col(3, h)], NT) * scale
            sig = 0.5 * jnp.tanh(0.5 * t) + 0.5
            p = t * sig
            p_ref[h, r, keys] = (p * mask_ref[r, keys]).astype(bf16)
            s_ref[h, r, keys] = (sig + p * (1.0 - sig)) * mask_ref[r, keys]
    project(1)
    project(0)
    load_cot.wait()
    for i in range(nblocks):
        r, keys, _ = spans(i)
        for h in range(HEADS):
            att_ref[r, head(h)] = mm(p_ref[h, r, keys], act_ref[keys, col(1, h)])
        _, in0, in1 = row_facts(i)
        att = att_ref[r, :]
        cen = att - jnp.mean(att, axis=1, keepdims=True)
        rstd = lax.rsqrt(jnp.mean(cen * cen, axis=1, keepdims=True) + 1e-05)
        z = cen * rstd
        up = jnp.where(in0 | in1, cot_ref[r, :].astype(jnp.float32), 0.0)
        dz = up * act_ref[r, section(0)].astype(jnp.float32)
        m1 = jnp.mean(dz, axis=1, keepdims=True)
        m2 = jnp.mean(dz * z, axis=1, keepdims=True)
        da_ref[r, :] = ((dz - m1 - z * m2) * rstd).astype(bf16)
        du = up * z
        att_ref[r, :] = up * z
    for j in range(HEADS // 2):
        store(0, j, send_ref, (1 - core) * (HEADS // 2) + j, pl.ds(0, rows), slope_ref, att_ref)
        store(0, j, keep_u_ref, core * (HEADS // 2) + j, pl.ds(0, rows), slope_ref, att_ref)
    backward(1 - core, send_ref, slope_ref, act_ref, p_ref, s_ref, ds_ref, da_ref)


def grads(lengths, x, w, cot):
    rows, d = x.shape
    width = cot.shape[1]
    wide = w.shape[1]
    vmem = pl.BlockSpec(memory_space=pltpu.VMEM)
    hbm = pl.BlockSpec(memory_space=pl.ANY)
    return pl.pallas_call(
        grads_kernel,
        out_shape=[
            pltpu.VMEM((rows, wide // 2), jnp.bfloat16),
            pltpu.VMEM((rows, width // 2), jnp.bfloat16),
            pltpu.VMEM((rows, wide), jnp.float32),
            pltpu.VMEM((rows, wide), jnp.bfloat16),
            pltpu.VMEM((HEADS, rows, rows), jnp.bfloat16),
            pltpu.VMEM((HEADS, rows, rows), jnp.float32),
            pltpu.VMEM((rows, width), jnp.bfloat16),
        ],
        in_specs=[hbm] * 4,
        out_specs=[vmem] * 7,
        scratch_shapes=[
            pltpu.SMEM((2,), jnp.int32),
            pltpu.VMEM((rows, d), jnp.bfloat16),
            pltpu.VMEM((d, wide), jnp.bfloat16),
            pltpu.VMEM((rows, width), jnp.bfloat16),
            pltpu.VMEM((rows, rows), jnp.float32),
            pltpu.VMEM((HEADS // 2, rows, rows), jnp.bfloat16),
            pltpu.VMEM((rows, width), jnp.float32),
            pltpu.SemaphoreType.DMA((7,)),
        ],
        compiler_params=pltpu.CompilerParams(vmem_limit_bytes=32 * 2**20),
        cost_estimate=pl.CostEstimate(flops=4 * 10**9, bytes_accessed=8 * 10**6, transcendentals=2 * 10**6),
        name="uvqk_grads",
    )(*[pltpu.with_memory_space_constraint(v, pltpu.HBM) for v in (lengths, x, w, cot)])


def flip(ref, out_ref):
    rows, d = ref.shape
    z = position()[3]
    for b in range(0, d, 256):
        for r in range(0, rows, 256):
            block = ref[pl.ds(r, 256), pl.ds(b, 256)].T
            for j in range(NZ):
                at = pl.multiple_of(b + (j ^ z) * 32, 32)
                out_ref[pl.ds(at, 32), pl.ds(r, 256)] = block[j * 32:(j + 1) * 32]


def blocks_of():
    y, core, x, _ = position()
    first = jnp.where(core == 0, x, y)
    second = jnp.where(core == 0, y, x)
    for k in range(4):
        for l in range(4):
            a = first ^ k
            b = second ^ l
            rb = jnp.where(core == 0, a, b)
            cb = jnp.where(core == 0, b, a)
            yield k, l, pl.ds(pl.multiple_of(rb * 256, 256), 256), pl.ds(pl.multiple_of(cb * 256, 256), 256)


def own_kernel(x_ref, theirs_ref, keep_u_ref, slope_ref, act_ref, p_ref, s_ref, da_ref,
               keep_ref, a0, a1, a2, a3, xt_ref, own_ref, ds_ref):
    flip(x_ref, own_ref)
    core = position()[1]
    keep_ref[:, pl.ds(0, keep_u_ref.shape[1])] = keep_u_ref[...]
    backward(core, keep_ref, slope_ref, act_ref, p_ref, s_ref, ds_ref, da_ref)
    sums = (a0, a1, a2, a3)
    for k, l, rs, cs in blocks_of():
        sums[k][l] = mm(own_ref[rs, :], keep_ref[:, cs])
    flip(theirs_ref, xt_ref)


def own_part(x, theirs, *state):
    rows, d = x.shape
    vmem = pl.BlockSpec(memory_space=pltpu.VMEM)
    return pl.pallas_call(
        own_kernel,
        out_shape=[pltpu.VMEM((rows, d), jnp.bfloat16)]
        + [pltpu.VMEM((4, 256, 256), jnp.float32)] * 4
        + [pltpu.VMEM((d, rows), jnp.bfloat16)],
        in_specs=[vmem] * 8,
        out_specs=[vmem] * 6,
        scratch_shapes=[
            pltpu.VMEM((d, rows), jnp.bfloat16),
            pltpu.VMEM((HEADS // 2, rows, rows), jnp.bfloat16),
        ],
        compiler_params=pltpu.CompilerParams(vmem_limit_bytes=32 * 2**20),
        cost_estimate=pl.CostEstimate(flops=14 * 10**8, bytes_accessed=20 * 2**20, transcendentals=0),
        name="own_weight_grads",
    )(x, theirs, *state)


def pair_kernel(ks, *refs):
    n = len(ks)
    xt_ref, recv_ref = refs[n:n + 2]
    for k, l, rs, cs in blocks_of():
        if k in ks:
            at = ks.index(k)
            total = refs[at][l] + mm(xt_ref[rs, :], recv_ref[:, cs])
            refs[n + 2 + at][l] = total.astype(jnp.bfloat16)


def pair_part(ks, sums, xt, recv):
    vmem = pl.BlockSpec(memory_space=pltpu.VMEM)
    n = len(ks)
    return pl.pallas_call(
        functools.partial(pair_kernel, ks),
        out_shape=[pltpu.VMEM((4, 256, 256), jnp.bfloat16)] * n,
        in_specs=[vmem] * (n + 2),
        out_specs=[vmem] * n,
        compiler_params=pltpu.CompilerParams(vmem_limit_bytes=24 * 2**20),
        cost_estimate=pl.CostEstimate(flops=n * 2**28, bytes_accessed=(2 * n + 2) * 2**20, transcendentals=0),
        name="pair_weight_grads",
    )(*[sums[k] for k in ks], xt, recv)


def rows_kernel(keep_ref, send_ref, w_ref, out_ref):
    core = position()[1]
    rows = keep_ref.shape[0]
    for r in range(0, rows, 256):
        total = jnp.zeros((256, w_ref.shape[0]), jnp.float32)
        for i, ref in enumerate((keep_ref, send_ref)):
            for s in range(4):
                cols = pl.ds(pl.multiple_of(s * 512 + (core ^ i) * 256, 256), 256)
                total += mm(ref[pl.ds(r, 256), pl.ds(s * 256, 256)], w_ref[:, cols], NT)
        out_ref[pl.ds(r, 256), :] = total.astype(jnp.bfloat16)


def row_grads(keep, send, w):
    vmem = pl.BlockSpec(memory_space=pltpu.VMEM)
    return pl.pallas_call(
        rows_kernel,
        out_shape=jax.ShapeDtypeStruct((keep.shape[0], w.shape[0]), jnp.bfloat16),
        in_specs=[vmem] * 3,
        out_specs=vmem,
        compiler_params=pltpu.CompilerParams(vmem_limit_bytes=24 * 2**20),
        cost_estimate=pl.CostEstimate(flops=2 * 2**30, bytes_accessed=7 * 2**20, transcendentals=0),
        name="row_grads",
    )(keep, send, w)


def place_kernel(p0, p1, p2, p3, out_ref):
    y, core, _, _ = position()
    for k, ref in enumerate((p0, p1, p2, p3)):
        s = y ^ k
        for i in range(2):
            cols = pl.ds(pl.multiple_of(s * 512 + (core ^ i) * 256, 256), 256)
            out_ref[:, cols] = ref[i].astype(jnp.float32)


def place(parts):
    vmem = pl.BlockSpec(memory_space=pltpu.VMEM)
    return pl.pallas_call(
        place_kernel,
        out_shape=jax.ShapeDtypeStruct((parts[0].shape[1], 2048), jnp.float32),
        in_specs=[vmem] * 4,
        out_specs=vmem,
        compiler_params=pltpu.CompilerParams(vmem_limit_bytes=4 * 2**20),
        name="place_columns",
    )(*parts)


def pairs(move):
    out = []
    for i in range(2 * NY * NX * NZ):
        g, m = divmod(i, NX * NZ)
        y, c = divmod(g, 2)
        x, z = divmod(m, NZ)
        y, c, x, z = move(y, c, x, z)
        out.append((i, ((y % NY) * 2 + c % 2) * NX * NZ + (x % NX) * NZ + z % NZ))
    return out


def permute(value, move):
    return lax.ppermute(value, AXES, pairs(move))


def other_core(y, c, x, z):
    return (y, c + 1, x, z)


def first_axis(k):
    return lambda y, c, x, z: (y, c, x ^ k, z) if c == 0 else (y ^ k, c, x, z)


def second_axis(k):
    return lambda y, c, x, z: (y ^ k, c, x, z) if c == 0 else (y, c, x ^ k, z)


def along_y(k):
    return lambda y, c, x, z: (y ^ k, c, x, z)


def along_z(k):
    return lambda y, c, x, z: (y, c, x, z ^ k)


def f32(value):
    return value.astype(jnp.float32)


def shards(histories, lengths, cotangent, w_in):
    theirs = permute(histories, other_core)
    send, *state = grads(lengths, histories, w_in, cotangent)
    recv = permute(send, other_core)
    keep, *sums, xt = own_part(histories, theirs, *state)
    far, = pair_part((2,), sums, xt, recv)
    near, = pair_part((1,), sums, xt, recv)
    last, = pair_part((3,), sums, xt, recv)
    moved = [permute(part, first_axis(k)) for k, part in ((2, far), (1, near), (3, last))]
    mine, = pair_part((0,), sums, xt, recv)
    grad_rows = row_grads(keep, send, w_in)
    *moved, mine, grad_rows = lax.optimization_barrier((*moved, mine, grad_rows))
    summed = [f32(mine[l]) + f32(moved[0][l]) + f32(moved[1][l]) + f32(moved[2][l]) for l in range(4)]
    moved = [permute(summed[k].astype(jnp.bfloat16), second_axis(k)) for k in (2, 1, 3)]
    block = summed[0] + f32(moved[0]) + f32(moved[1]) + f32(moved[2])
    block = block.reshape(NZ, 32, 256)
    ends = jnp.stack([block[0], block[7]])
    moved = [permute(jnp.stack([block[m], block[7 - m]]).astype(jnp.bfloat16), along_z(m)) for m in (1, 3, 2)]
    ends = ends + f32(moved[0]) + f32(moved[1]) + f32(moved[2])
    block = ends[0] + permute(ends[1], along_z(7))

    block = block.astype(jnp.bfloat16)
    both = jnp.stack([block, permute(block, other_core)])
    gathered = {k: permute(both, along_y(k)) for k in (2, 1, 3)}
    grad_w = place([both, gathered[1], gathered[2], gathered[3]])
    return (grad_rows, grad_w)


def solution(mesh):
    return jax.shard_map(
        shards,
        mesh=mesh,
        in_specs=(
            P(("group", "member"), None),
            P(("group", "member")),
            P(("group", "member"), None),
            P(),
        ),
        out_specs=(P(("group", "member"), None), P("member", None)),
        check_vma=False,
    )
```

```python
import functools

import jax
import jax.numpy as jnp
from jax import lax
from jax.sharding import PartitionSpec as P
from jax.experimental import pallas as pl
from jax.experimental.pallas import tpu as pltpu

HEADS = 4
BLOCK = 128
AXES = ("group", "member")
NY, NX, NZ = 4, 4, 8
NT = (((1,), (1,)), ((), ()))
TN = (((0,), (0,)), ((), ()))


def mm(a, b, dims=(((1,), (0,)), ((), ()))):
    return lax.dot_general(a, b, dims, preferred_element_type=jnp.float32)


def position():
    group, member = lax.axis_index("group"), lax.axis_index("member")
    return group // 2, group % 2, member // NZ, member % NZ


def spans(i):
    first = max(0, i - 2)
    return pl.ds(i * BLOCK, BLOCK), pl.ds(first * BLOCK, (i + 1 - first) * BLOCK), first


def col(s, h):
    return pl.ds(pl.multiple_of((s * HEADS + h) * BLOCK, BLOCK), BLOCK)


def head(h):
    return col(0, h)


def store(s, j, out_ref, h, r, slope_ref, grad):
    if s == 0:
        grad = grad[r, head(h)]
    value = grad.astype(jnp.bfloat16).astype(jnp.float32) * slope_ref[r, col(s, h)]
    out_ref[r, pl.ds((s * (HEADS // 2) + j) * BLOCK, BLOCK)] = value.astype(jnp.bfloat16)


def backward(side, out_ref, slope_ref, act_ref, p_ref, s_ref, ds_ref, da_ref):
    nblocks = act_ref.shape[0] // BLOCK
    scale = BLOCK ** -0.5
    heads = [(j, side * (HEADS // 2) + j) for j in range(HEADS // 2)]
    for i in range(nblocks):
        r, keys, _ = spans(i)
        for j, h in heads:
            dp = mm(da_ref[r, head(h)], act_ref[keys, col(1, h)], NT)
            ds_ref[j, r, keys] = (dp * s_ref[h, r, keys]).astype(jnp.bfloat16)
    for i in range(nblocks):
        r, keys, _ = spans(i)
        for j, h in heads:
            dq = mm(ds_ref[j, r, keys], act_ref[keys, col(3, h)]) * scale
            store(2, j, out_ref, h, r, slope_ref, dq)
    for b in range(nblocks):
        last = min(nblocks, b + 3)
        r = pl.ds(b * BLOCK, BLOCK)
        qs = pl.ds(b * BLOCK, (last - b) * BLOCK)
        for j, h in heads:
            dv = mm(p_ref[h, qs, r], da_ref[qs, head(h)], TN)
            store(1, j, out_ref, h, r, slope_ref, dv)
            dk = mm(ds_ref[j, qs, r], act_ref[qs, col(2, h)], TN) * scale
            store(3, j, out_ref, h, r, slope_ref, dk)


def grads_kernel(len_hbm, x_hbm, w_hbm, cot_hbm, send_ref, keep_u_ref, slope_ref, act_ref, p_ref, s_ref, da_ref,
                 len_ref, x_ref, w_ref, cot_ref, mask_ref, ds_ref, att_ref, sems):
    rows, width = cot_ref.shape
    nblocks = rows // BLOCK
    size = width // HEADS
    half = width // 2
    scale = size ** -0.5
    bf16 = jnp.bfloat16

    def section(s):
        return pl.ds(s * width, width)

    loads = {s: pltpu.make_async_copy(w_hbm.at[:, section(s)], w_ref.at[:, section(s)], sems.at[s])
             for s in range(4)}
    load_x = pltpu.make_async_copy(x_hbm, x_ref, sems.at[4])
    load_cot = pltpu.make_async_copy(cot_hbm, cot_ref, sems.at[5])
    load_len = pltpu.make_async_copy(len_hbm, len_ref, sems.at[6])
    load_len.start()
    load_x.start()
    loads[2].start()
    loads[3].start()
    load_len.wait()

    l0 = len_ref[0]
    l1 = len_ref[1]
    start1 = ((l0 + (BLOCK - 1)) // BLOCK) * BLOCK

    def row_facts(i):
        row = i * BLOCK + lax.broadcasted_iota(jnp.int32, (BLOCK, 1), 0)
        in0 = row < l0
        in1 = (row >= start1) & (row < start1 + l1)
        return row, in0, in1

    for i in range(nblocks):
        r, keys, first = spans(i)
        row, in0, in1 = row_facts(i)
        low = jnp.where(in1, start1, 0)
        high = jnp.where(in0 | in1, row, -1)
        count = jnp.where(in0, l0, jnp.where(in1, l1, 1))
        inv = 1.0 / count.astype(jnp.float32)
        c = first * BLOCK + lax.broadcasted_iota(jnp.int32, (BLOCK, keys.size), 1)
        mask_ref[r, keys] = jnp.where((c >= low) & (c <= high), inv, 0.0)

    def project(s):
        loads[s].wait()
        h = mm(x_ref[...], w_ref[:, section(s)])
        sig = 0.5 * jnp.tanh(0.5 * h) + 0.5
        act = h * sig
        act_ref[:, section(s)] = act.astype(bf16)
        slope_ref[:, section(s)] = sig + act * (1.0 - sig)

    core = position()[1]

    load_x.wait()
    loads[1].start()
    project(2)
    loads[0].start()
    load_cot.start()
    project(3)
    for i in range(nblocks):
        r, keys, _ = spans(i)
        for h in range(HEADS):
            t = mm(act_ref[r, col(2, h)], act_ref[keys, col(3, h)], NT) * scale
            sig = 0.5 * jnp.tanh(0.5 * t) + 0.5
            p = t * sig
            p_ref[h, r, keys] = (p * mask_ref[r, keys]).astype(bf16)
            s_ref[h, r, keys] = (sig + p * (1.0 - sig)) * mask_ref[r, keys]
    project(1)
    project(0)
    load_cot.wait()
    for i in range(nblocks):
        r, keys, _ = spans(i)
        for h in range(HEADS):
            att_ref[r, head(h)] = mm(p_ref[h, r, keys], act_ref[keys, col(1, h)])
        _, in0, in1 = row_facts(i)
        att = att_ref[r, :]
        cen = att - jnp.mean(att, axis=1, keepdims=True)
        rstd = lax.rsqrt(jnp.mean(cen * cen, axis=1, keepdims=True) + 1e-05)
        z = cen * rstd
        up = jnp.where(in0 | in1, cot_ref[r, :].astype(jnp.float32), 0.0)
        dz = up * act_ref[r, section(0)].astype(jnp.float32)
        m1 = jnp.mean(dz, axis=1, keepdims=True)
        m2 = jnp.mean(dz * z, axis=1, keepdims=True)
        da_ref[r, :] = ((dz - m1 - z * m2) * rstd).astype(bf16)
        du = up * z
        att_ref[r, :] = up * z
    for j in range(HEADS // 2):
        store(0, j, send_ref, (1 - core) * (HEADS // 2) + j, pl.ds(0, rows), slope_ref, att_ref)
        store(0, j, keep_u_ref, core * (HEADS // 2) + j, pl.ds(0, rows), slope_ref, att_ref)
    backward(1 - core, send_ref, slope_ref, act_ref, p_ref, s_ref, ds_ref, da_ref)


def grads(lengths, x, w, cot):
    rows, d = x.shape
    width = cot.shape[1]
    wide = w.shape[1]
    vmem = pl.BlockSpec(memory_space=pltpu.VMEM)
    hbm = pl.BlockSpec(memory_space=pl.ANY)
    return pl.pallas_call(
        grads_kernel,
        out_shape=[
            pltpu.VMEM((rows, wide // 2), jnp.bfloat16),
            pltpu.VMEM((rows, width // 2), jnp.bfloat16),
            pltpu.VMEM((rows, wide), jnp.float32),
            pltpu.VMEM((rows, wide), jnp.bfloat16),
            pltpu.VMEM((HEADS, rows, rows), jnp.bfloat16),
            pltpu.VMEM((HEADS, rows, rows), jnp.float32),
            pltpu.VMEM((rows, width), jnp.bfloat16),
        ],
        in_specs=[hbm] * 4,
        out_specs=[vmem] * 7,
        scratch_shapes=[
            pltpu.SMEM((2,), jnp.int32),
            pltpu.VMEM((rows, d), jnp.bfloat16),
            pltpu.VMEM((d, wide), jnp.bfloat16),
            pltpu.VMEM((rows, width), jnp.bfloat16),
            pltpu.VMEM((rows, rows), jnp.float32),
            pltpu.VMEM((HEADS // 2, rows, rows), jnp.bfloat16),
            pltpu.VMEM((rows, width), jnp.float32),
            pltpu.SemaphoreType.DMA((7,)),
        ],
        compiler_params=pltpu.CompilerParams(vmem_limit_bytes=32 * 2**20),
        cost_estimate=pl.CostEstimate(flops=4 * 10**9, bytes_accessed=8 * 10**6, transcendentals=2 * 10**6),
        name="uvqk_grads",
    )(*[pltpu.with_memory_space_constraint(v, pltpu.HBM) for v in (lengths, x, w, cot)])


def flip(ref, out_ref):
    rows, d = ref.shape
    z = position()[3]
    for b in range(0, d, 256):
        for r in range(0, rows, 256):
            block = ref[pl.ds(r, 256), pl.ds(b, 256)].T
            for j in range(NZ):
                at = pl.multiple_of(b + (j ^ z) * 32, 32)
                out_ref[pl.ds(at, 32), pl.ds(r, 256)] = block[j * 32:(j + 1) * 32]


def blocks_of():
    y, core, x, _ = position()
    first = jnp.where(core == 0, x, y)
    second = jnp.where(core == 0, y, x)
    for k in range(4):
        for l in range(4):
            a = first ^ k
            b = second ^ l
            rb = jnp.where(core == 0, a, b)
            cb = jnp.where(core == 0, b, a)
            yield k, l, pl.ds(pl.multiple_of(rb * 256, 256), 256), pl.ds(pl.multiple_of(cb * 256, 256), 256)


def own_kernel(x_ref, theirs_ref, keep_u_ref, slope_ref, act_ref, p_ref, s_ref, da_ref,
               keep_ref, a0, a1, a2, a3, xt_ref, own_ref, ds_ref):
    flip(x_ref, own_ref)
    core = position()[1]
    keep_ref[:, pl.ds(0, keep_u_ref.shape[1])] = keep_u_ref[...]
    backward(core, keep_ref, slope_ref, act_ref, p_ref, s_ref, ds_ref, da_ref)
    sums = (a0, a1, a2, a3)
    for k, l, rs, cs in blocks_of():
        sums[k][l] = mm(own_ref[rs, :], keep_ref[:, cs])
    flip(theirs_ref, xt_ref)


def own_part(x, theirs, *state):
    rows, d = x.shape
    vmem = pl.BlockSpec(memory_space=pltpu.VMEM)
    return pl.pallas_call(
        own_kernel,
        out_shape=[pltpu.VMEM((rows, d), jnp.bfloat16)]
        + [pltpu.VMEM((4, 256, 256), jnp.float32)] * 4
        + [pltpu.VMEM((d, rows), jnp.bfloat16)],
        in_specs=[vmem] * 8,
        out_specs=[vmem] * 6,
        scratch_shapes=[
            pltpu.VMEM((d, rows), jnp.bfloat16),
            pltpu.VMEM((HEADS // 2, rows, rows), jnp.bfloat16),
        ],
        compiler_params=pltpu.CompilerParams(vmem_limit_bytes=32 * 2**20),
        cost_estimate=pl.CostEstimate(flops=14 * 10**8, bytes_accessed=20 * 2**20, transcendentals=0),
        name="own_weight_grads",
    )(x, theirs, *state)


def pair_kernel(ks, *refs):
    n = len(ks)
    xt_ref, recv_ref = refs[n:n + 2]
    for k, l, rs, cs in blocks_of():
        if k in ks:
            at = ks.index(k)
            total = refs[at][l] + mm(xt_ref[rs, :], recv_ref[:, cs])
            refs[n + 2 + at][l] = total.astype(jnp.bfloat16)


def pair_part(ks, sums, xt, recv):
    vmem = pl.BlockSpec(memory_space=pltpu.VMEM)
    n = len(ks)
    return pl.pallas_call(
        functools.partial(pair_kernel, ks),
        out_shape=[pltpu.VMEM((4, 256, 256), jnp.bfloat16)] * n,
        in_specs=[vmem] * (n + 2),
        out_specs=[vmem] * n,
        compiler_params=pltpu.CompilerParams(vmem_limit_bytes=24 * 2**20),
        cost_estimate=pl.CostEstimate(flops=n * 2**28, bytes_accessed=(2 * n + 2) * 2**20, transcendentals=0),
        name="pair_weight_grads",
    )(*[sums[k] for k in ks], xt, recv)


def rows_kernel(keep_ref, send_ref, w_ref, out_ref):
    core = position()[1]
    rows = keep_ref.shape[0]
    for r in range(0, rows, 256):
        total = jnp.zeros((256, w_ref.shape[0]), jnp.float32)
        for i, ref in enumerate((keep_ref, send_ref)):
            for s in range(4):
                cols = pl.ds(pl.multiple_of(s * 512 + (core ^ i) * 256, 256), 256)
                total += mm(ref[pl.ds(r, 256), pl.ds(s * 256, 256)], w_ref[:, cols], NT)
        out_ref[pl.ds(r, 256), :] = total.astype(jnp.bfloat16)


def row_grads(keep, send, w):
    vmem = pl.BlockSpec(memory_space=pltpu.VMEM)
    return pl.pallas_call(
        rows_kernel,
        out_shape=jax.ShapeDtypeStruct((keep.shape[0], w.shape[0]), jnp.bfloat16),
        in_specs=[vmem] * 3,
        out_specs=vmem,
        compiler_params=pltpu.CompilerParams(vmem_limit_bytes=24 * 2**20),
        cost_estimate=pl.CostEstimate(flops=2 * 2**30, bytes_accessed=7 * 2**20, transcendentals=0),
        name="row_grads",
    )(keep, send, w)


def place_kernel(p0, p1, p2, p3, out_ref):
    y, core, _, _ = position()
    for k, ref in enumerate((p0, p1, p2, p3)):
        s = y ^ k
        for i in range(2):
            cols = pl.ds(pl.multiple_of(s * 512 + (core ^ i) * 256, 256), 256)
            out_ref[:, cols] = ref[i].astype(jnp.float32)


def place(parts):
    vmem = pl.BlockSpec(memory_space=pltpu.VMEM)
    return pl.pallas_call(
        place_kernel,
        out_shape=jax.ShapeDtypeStruct((parts[0].shape[1], 2048), jnp.float32),
        in_specs=[vmem] * 4,
        out_specs=vmem,
        compiler_params=pltpu.CompilerParams(vmem_limit_bytes=4 * 2**20),
        name="place_columns",
    )(*parts)


def pairs(move):
    out = []
    for i in range(2 * NY * NX * NZ):
        g, m = divmod(i, NX * NZ)
        y, c = divmod(g, 2)
        x, z = divmod(m, NZ)
        y, c, x, z = move(y, c, x, z)
        out.append((i, ((y % NY) * 2 + c % 2) * NX * NZ + (x % NX) * NZ + z % NZ))
    return out


def permute(value, move):
    return lax.ppermute(value, AXES, pairs(move))


def other_core(y, c, x, z):
    return (y, c + 1, x, z)


def first_axis(k):
    return lambda y, c, x, z: (y, c, x ^ k, z) if c == 0 else (y ^ k, c, x, z)


def second_axis(k):
    return lambda y, c, x, z: (y ^ k, c, x, z) if c == 0 else (y, c, x ^ k, z)


def along_y(k):
    return lambda y, c, x, z: (y ^ k, c, x, z)


def along_z(k):
    return lambda y, c, x, z: (y, c, x, z ^ k)


def f32(value):
    return value.astype(jnp.float32)


def shards(histories, lengths, cotangent, w_in):
    theirs = permute(histories, other_core)
    send, *state = grads(lengths, histories, w_in, cotangent)
    recv = permute(send, other_core)
    keep, *sums, xt = own_part(histories, theirs, *state)
    far, = pair_part((2,), sums, xt, recv)
    near, = pair_part((1,), sums, xt, recv)
    last, = pair_part((3,), sums, xt, recv)
    moved = [permute(part, first_axis(k)) for k, part in ((2, far), (1, near), (3, last))]
    mine, = pair_part((0,), sums, xt, recv)
    grad_rows = row_grads(keep, send, w_in)
    *moved, mine, grad_rows = lax.optimization_barrier((*moved, mine, grad_rows))
    summed = [f32(mine[l]) + f32(moved[0][l]) + f32(moved[1][l]) + f32(moved[2][l]) for l in range(4)]
    moved = [permute(summed[k].astype(jnp.bfloat16), second_axis(k)) for k in (2, 1, 3)]
    block = summed[0] + f32(moved[0]) + f32(moved[1]) + f32(moved[2])
    block = block.reshape(NZ, 32, 256)
    ends = jnp.stack([block[0], block[7]])
    moved = [permute(jnp.stack([block[m], block[7 - m]]).astype(jnp.bfloat16), along_z(m)) for m in (1, 3, 2)]
    ends = ends + f32(moved[0]) + f32(moved[1]) + f32(moved[2])
    block = ends[0] + f32(permute(ends[1].astype(jnp.bfloat16), along_z(7)))

    block = block.astype(jnp.bfloat16)
    both = jnp.stack([block, permute(block, other_core)])
    gathered = {k: permute(both, along_y(k)) for k in (2, 1, 3)}
    grad_w = place([both, gathered[1], gathered[2], gathered[3]])
    return (grad_rows, grad_w)


def solution(mesh):
    return jax.shard_map(
        shards,
        mesh=mesh,
        in_specs=(
            P(("group", "member"), None),
            P(("group", "member")),
            P(("group", "member"), None),
            P(),
        ),
        out_specs=(P(("group", "member"), None), P("member", None)),
        check_vma=False,
    )
```
